32 devices in a mesh: lon: 8 (over z, x), lat: 4 (over y, core).
Axes of the slice: x: 2, y: 2, z: 4, core: 2. Of those that a mesh axis runs over, the one named last changes fastest.
Arguments:
- model_variables: float32 [3, 64, 32, 1024], P(None, None, 'lat', 'lon'), may hold values from -6 to 6
- obs_cell: int32 [2, 64], replicated, may hold values from 0 to 32767
- obs_value: float32 [2, 64], replicated, may hold values from -8 to 8
- obs_variance: float32 [2, 64], replicated, may hold values from 0.2 to 2
- tile_mask: int32 [2, 64, 32], P(None, None, ('lon', 'lat')), may hold values 0 or 1
Outputs:
- analysis: float32 [3, 64, 32, 1024], P(None, None, 'lat', 'lon')
The draws below stay inside these ranges and needn't reach their ends.
All inputs are finite; a program needn't handle non-finite values. No bound on the sum of `tile_mask` on one device may be relied on, other than what follows from the above.
Results may differ from the reference program's by a relative error of at most 0.00015.
Values sent between devices are 32-bit elements; how exact they have to be, the bound alone decides.
No kernel may reach another device: no remote copies, remote signals or barrier semaphores. Data moves between devices by JAX's collectives and lax.ppermute only.
A program may use at most 64 MiB of HBM per device.

```python
import math
import jax
import jax.numpy as jnp
from jax import lax

MEMBERS = 64
LAT_DEV = 8
LON_DEV = 128
STEPS = 4
NBATCH = 2
NOBS = 64
NLAT = 32
NLON = 1024
NTILES = 32
LOC_RADIUS = 256
N_LON = 8
N_LAT = 4


def touch_ends(drawn, rng, smallest, top_value):
    place = [jax.random.randint(jax.random.fold_in(rng, axis), (), 0, length) for axis, length in enumerate(drawn.shape)]
    longest = drawn.shape.index(max(drawn.shape))
    beside = place[:longest] + [(place[longest] + 1) % drawn.shape[longest]] + place[longest + 1:]
    return drawn.at[tuple(place)].set(smallest).at[tuple(beside)].set(top_value)


def steps_of(stream_key, extent, split, low, high):
    def one(position, blocks):
        draws = jax.random.uniform(jax.random.fold_in(jax.random.fold_in(stream_key, 6), position), (blocks,), jnp.float32, low / len(split), high / len(split))
        return jnp.repeat(jnp.exp(draws), extent[position] // blocks).reshape((-1,) + (1,) * (len(extent) - position - 1))

    level = one(*split[0])
    for cut in split[1:]:
        level = level * one(*cut)
    return level


def centred(stream_key, extent, deviation, limit, cuts=(), kind=jnp.bfloat16):
    result = jax.random.normal(stream_key, extent, jnp.float32) * deviation
    if len(cuts) > 0:
        result = steps_of(stream_key, extent, cuts, -0.22, 0.18) * result
    return jnp.clip(result, min=-limit, max=limit).astype(kind)


def setup_inputs(seed: int = 0) -> dict:
    streams_of = jax.random.split(jax.random.key(seed), 6)
    model_variables = centred(streams_of[0], (3, MEMBERS, NLAT, NLON), 1.0, 6.0, ((2, 4), (3, 8)), jnp.float32)
    obs_cell = touch_ends(jax.random.randint(streams_of[1], (NBATCH, NOBS), 0, NLAT * NLON), jax.random.fold_in(streams_of[1], 1), 0, (NLAT * NLON) - 1).astype(jnp.int32)
    obs_value = centred(streams_of[2], (NBATCH, NOBS), 1.5, 8.0, (), jnp.float32)
    obs_variance = jnp.clip(jnp.exp(jax.random.uniform(streams_of[3], (NBATCH, NOBS), jnp.float32, math.log(0.2), math.log(2.0))), 0.2, 2.0)
    tile_mask = touch_ends((jax.random.randint(streams_of[4], (NBATCH, NOBS, NTILES), 0, 4) < 3).astype(jnp.int32), jax.random.fold_in(streams_of[4], 1), 0, 1)
    return dict(model_variables=model_variables, obs_cell=obs_cell, obs_value=obs_value, obs_variance=obs_variance, tile_mask=tile_mask)


CORIOLIS = 0.1
COURANT = 0.5
SMALL_EPSILON = 1e-06

def east_diff(field):
    return 0.5 * (jnp.roll(field, -1, axis=-1) - jnp.roll(field, 1, axis=-1))

def north_diff(field):
    padded = jnp.pad(field, ((1, 1), (0, 0)))
    return 0.5 * (padded[2:] - padded[:-2])

def single_prediction(layered_arrays):
    surface_elevation, east, north = (layered_arrays[0], layered_arrays[1], layered_arrays[2])
    rows = jnp.arange(NLAT, dtype=jnp.int32).astype(jnp.float32)
    coriolis = (CORIOLIS * ((2.0 * rows + 1.0) / NLAT - 1.0))[:, None]
    for step in range(STEPS):
        surface_elevation = surface_elevation - COURANT * (east_diff(east) + north_diff(north))
        east_next = east + coriolis * north - COURANT * east_diff(surface_elevation)
        north = north - coriolis * east - COURANT * north_diff(surface_elevation)
        east = east_next
    return jnp.stack([surface_elevation, east, north])

def increments(prior, value, variance):
    center = jnp.mean(prior)
    spread_dev = prior - center
    spread = jnp.sum(spread_dev * spread_dev) / (MEMBERS - 1) + SMALL_EPSILON
    post = 1.0 / (1.0 / spread + 1.0 / variance)
    post_mean = post * (center / spread + value / variance)
    delta = post_mean - center + (jnp.sqrt(post / spread) - 1.0) * spread_dev
    slope = spread_dev / ((MEMBERS - 1) * spread)
    return (delta, slope)

def tile_weights(cells, mask_batch):
    obs_lat = cells // NLON
    obs_lon = cells % NLON
    tiles = jnp.arange(N_LON * N_LAT, dtype=jnp.int32)
    centre_lat = tiles % N_LAT * LAT_DEV + LAT_DEV // 2
    central_longitude = tiles // N_LAT * LON_DEV + LON_DEV // 2
    lat_gap = obs_lat[:, None] - centre_lat[None, :]
    lon_gap = jnp.abs(obs_lon[:, None] - central_longitude[None, :])
    lon_gap = jnp.minimum(lon_gap, NLON - lon_gap)
    distance = (lat_gap * lat_gap + lon_gap * lon_gap).astype(jnp.float32)
    return mask_batch.astype(jnp.float32) / (1.0 + distance / (LOC_RADIUS * LOC_RADIUS))

def assimilate(model_variables, cells, values, variances, weights):
    surface_elevation = model_variables[0]
    obs_lat = cells // NLON
    obs_lon = cells % NLON
    priors = jnp.transpose(surface_elevation[:, obs_lat, obs_lon])
    owning_patch = obs_lon // LON_DEV * N_LAT + obs_lat // LAT_DEV
    links = jnp.transpose(weights[:, owning_patch])
    tiles = N_LON * N_LAT
    transforms = jnp.broadcast_to(jnp.eye(MEMBERS, dtype=jnp.float32), (tiles, MEMBERS, MEMBERS))

    def turn(k, carry):
        priors, transforms = carry
        delta, slope = increments(priors[k], values[k], variances[k])
        coef = links[:, k] * jnp.dot(priors, slope, precision=lax.Precision.HIGHEST)
        priors = priors + coef[:, None] * delta[None, :]
        lifted = jnp.einsum('tmn,n->tm', transforms, slope, precision=lax.Precision.HIGHEST)
        transforms = transforms + weights[k][:, None, None] * lifted[:, :, None] * delta[None, None, :]
        return (priors, transforms)
    priors, transforms = lax.fori_loop(0, NOBS, turn, (priors, transforms))
    grid = transforms.reshape(N_LON, N_LAT, MEMBERS, MEMBERS)
    tiled = model_variables.reshape(3, MEMBERS, N_LAT, LAT_DEV, N_LON, LON_DEV)
    tiled = jnp.moveaxis(tiled, 4, 0)

    def apply_column(pair):
        block, mats = pair
        return jnp.einsum('fmaij,amn->fnaij', block, mats, precision=lax.Precision.HIGHEST)
    updated = lax.map(apply_column, (tiled, grid))
    return jnp.moveaxis(updated, 0, 4).reshape(model_variables.shape)

def reference(model_variables, obs_cell, obs_value, obs_variance, tile_mask):
    ensemble_snapshots = lax.map(single_prediction, jnp.moveaxis(model_variables, 1, 0))
    model_variables = jnp.moveaxis(ensemble_snapshots, 0, 1)
    for batch in range(NBATCH):
        cells = obs_cell[batch]
        weights = tile_weights(cells, tile_mask[batch])
        model_variables = assimilate(model_variables, cells, obs_value[batch], obs_variance[batch], weights)
    return model_variables
```

```python
import functools
import math

import jax
import jax.numpy as jnp
from jax import lax
from jax.experimental import pallas as pl
from jax.experimental.pallas import tpu as pltpu
from jax.sharding import PartitionSpec as P

STEPS = 4
NBATCH = 2
LOC_RADIUS = 256

CORIOLIS = 0.1
COURANT = 0.5
SMALL_EPSILON = 1e-06

SUB = 8
LANES = 128
STRIP = 8
PANEL = 4
JOINED = 4
PICKS = 4
HIGHEST = lax.Precision.HIGHEST
VMEM_LIMIT = 48 * 1024 * 1024
FORECAST_LIMIT = 53 * 1024 * 1024 + 320 * 1024


def dot(a, b):
    return jnp.dot(a, b, precision=HIGHEST, preferred_element_type=jnp.float32)


def dot_rows(a, b):
    return lax.dot_general(
        a, b, (((0,), (0,)), ((), ())), precision=HIGHEST, preferred_element_type=jnp.float32
    )


def forecast_kernel(
    groups, members, n_lat, n_lon, cell_hbm, mask_hbm, own_hbm,
    core_out, mid_out, cross_out, core_strip, mid_strip, cross_strip, share_ref, cell_out,
    heights, slots, state, cell_ref, mask_ref, own_ref, parts, up_strip, down_strip, small_sems, own_sems, out_sems,
):
    lat = lax.axis_index("lat")
    lon = lax.axis_index("lon")
    odd = lax.rem(lat, 2)
    total_rows = n_lat * SUB
    total_cols = n_lon * LANES
    lane = lax.broadcasted_iota(jnp.int32, (SUB, LANES), 1)
    scales, turns = [], []
    for row in range(-SUB, 2 * SUB):
        place = lat * SUB + row
        inside = jnp.logical_and(place >= 0, place < total_rows)
        spin = CORIOLIS * ((2.0 * place.astype(jnp.float32) + 1.0) / total_rows - 1.0)
        scales.append(jnp.where(inside, 0.5 * COURANT, 0.0))
        turns.append(jnp.where(inside, spin, 0.0))
    batches, count = cell_ref.shape
    slice_size = batches * count * JOINED // groups
    share_rows = SUB * SUB * JOINED

    def own_copy(turn):
        rows = pl.ds(pl.multiple_of(turn * share_rows, share_rows), share_rows)
        return pltpu.make_async_copy(own_hbm.at[:, rows], own_ref.at[:, rows], own_sems.at[turn])

    def part_copies(turn, rows):
        return [
            pltpu.make_async_copy(parts.at[part, :, :, rows], out.at[:, :, rows], out_sems.at[turn, place])
            for place, (part, out) in enumerate(((2 - 2 * odd, core_out), (1, mid_out), (2 * odd, cross_out)))
        ]

    def group_rows(turn):
        return pl.ds(pl.multiple_of(turn * SUB * JOINED, SUB * JOINED), SUB * JOINED)

    small = [
        pltpu.make_async_copy(source, target, small_sems.at[place])
        for place, (source, target) in enumerate((
            (cell_hbm, cell_ref), (cell_hbm, cell_out), (mask_hbm, mask_ref)
        ))
    ]
    own_copy(0).start()
    for copy in small:
        copy.start()
    for turn in range(1, groups // JOINED):
        own_copy(turn).start()
    for copy in small:
        copy.wait()

    def minus(a, b):
        if b is None:
            return a
        return -b if a is None else a - b

    def plus(a, b):
        if a is None or b is None:
            return b if a is None else a
        return a + b

    def times(scale, a):
        return None if a is None else scale * a

    def along(x):
        if x is None:
            return None
        return pltpu.roll(x, 2 * LANES - 1, 1) - pltpu.roll(x, 1, 1)

    def member_groups(turn, found):
        own_copy(turn).wait()
        first = turn * JOINED
        live = [dict() for _ in range(3)]

        def get(field, row):
            return state[field, row + SUB] if row in live[field] else None

        def put(field, row, value):
            if value is not None:
                live[field][row] = True
                state[field, row + SUB] = value

        for field in range(3):
            for row in range(SUB):
                pieces = [
                    own_ref[field, pl.ds((first + group) * SUB * SUB + row, SUB, stride=SUB), :]
                    for group in range(JOINED)
                ]
                main = jnp.concatenate(pieces, axis=0)
                put(field, row, jnp.concatenate([main, jnp.zeros_like(main)], axis=1))
        for step in range(STEPS):
            for row in range(-SUB, 2 * SUB):
                slope = plus(along(get(1, row)), minus(get(2, row + 1), get(2, row - 1)))
                put(0, row, minus(get(0, row), times(scales[row + SUB], slope)))
            for row in range(-SUB, 2 * SUB):
                east, north = get(1, row), get(2, row)
                slope = minus(get(0, row + 1), get(0, row - 1))
                put(1, row, minus(plus(east, times(turns[row + SUB], north)), times(scales[row + SUB], along(get(0, row)))))
                put(2, row, minus(minus(north, times(turns[row + SUB], east)), times(scales[row + SUB], slope)))

        for row in range(-SUB, 2 * SUB):
            part = row // SUB + 1
            for field in range(3):
                value = get(field, row)
                if value is None:
                    value = jnp.zeros((SUB * JOINED, 2 * LANES), jnp.float32)
                place = group_rows(turn)
                parts[part, field, row % SUB, place, :] = value[:, :LANES]
                strips = (up_strip, mid_strip, down_strip)[part]
                strip = strips[field, row % SUB]
                for group in range(JOINED):
                    halo = value[SUB * group:SUB * (group + 1), LANES:]
                    turned = pltpu.roll(halo, 2 * STRIP * (first + group) + STRIP, 1)
                    strip = jnp.where(lane // (2 * STRIP) == first + group, turned, strip)
                strips[field, row % SUB] = strip
                if field == 0:
                    heights[row + SUB, 0, place, :] = value[:, :LANES]
                    heights[row + SUB, 1, place, :] = value[:, LANES:]
        for copy in part_copies(turn, group_rows(turn)):
            copy.start()
        for extra in range(slice_size):
            index = turn * slice_size + extra
            cell = cell_ref[lax.div(index, count), lax.rem(index, count)]
            row = lax.div(cell, total_cols)
            col = cell - row * total_cols - lon * LANES
            row = row - lat * SUB + SUB
            col = jnp.where(col < 0, col + total_cols, col)
            west = col >= total_cols - STRIP
            near = jnp.logical_and(row > 0, row < 3 * SUB - 1)
            near = jnp.logical_and(near, jnp.logical_or(col < LANES + STRIP, west))
            ring = jnp.where(west, col + (2 * LANES - total_cols), col)
            slots[found] = (row * (2 * LANES) + ring) * LANES + index
            found = found + near.astype(jnp.int32)
        return found

    found = lax.fori_loop(0, groups // JOINED, member_groups, 0)
    core_strip[...] = jnp.where(odd == 1, up_strip[...], down_strip[...])
    cross_strip[...] = jnp.where(odd == 1, down_strip[...], up_strip[...])
    tiles = share_ref.shape[0] - members
    mine = lax.broadcasted_iota(jnp.int32, (tiles, LANES), 0) == lax.rem(lon * n_lat + lat, tiles)
    mask = jnp.concatenate([mask_ref[batch] for batch in range(batches)], axis=1).astype(jnp.float32)
    share_ref[members:, :] = jnp.where(mine, mask, 0.0)
    wide = lax.broadcasted_iota(jnp.int32, (members, LANES), 1)

    def pick(turn, share):
        for extra in range(PICKS):
            item = turn * PICKS + extra
            packed = jnp.where(item < found, slots[item], 0)
            index = packed & (LANES - 1)
            col = (packed >> 7) & (LANES - 1)
            slab = heights[packed >> 15, (packed >> 14) & 1]
            turned = pltpu.roll(slab, (index - col) & (LANES - 1), 1)
            share = jnp.where(wide == jnp.where(item < found, index, LANES), turned, share)
        return share

    share_ref[:members, :] = lax.fori_loop(
        0, lax.div(found + PICKS - 1, PICKS), pick, jnp.zeros((members, LANES), jnp.float32)
    )
    for turn in range(groups // JOINED):
        for copy in part_copies(turn, group_rows(turn)):
            copy.wait()


def batch_steps(
    values, variances, batch, count, own, other, lam_own, lam_other, lam_cols, offset, mean, spin,
    hist_other, hist_rows,
):
    groups = count // SUB
    own = [own[SUB * i:SUB * (i + 1)] for i in range(groups)]
    other = [other[SUB * i:SUB * (i + 1)] for i in range(groups)]

    def spread(x, row):
        return jnp.broadcast_to(x[row:row + 1], (SUB, LANES))

    def column(x, lane):
        return jnp.broadcast_to(x[:, lane:lane + 1], (SUB, LANES))

    for first in range(0, count, PANEL):
        home, base = divmod(first, SUB)
        live = range(home, groups)
        inside = range(PANEL)
        cols = [{i: column(own[i], first + q) for i in live} for q in inside]
        lams = [
            {i: column(lam_cols[SUB * i:SUB * (i + 1)], offset + first + q) for i in live} for q in inside
        ]
        block = {(a, b): spread(cols[b][home], base + a) for a in inside for b in inside if a <= b}
        means = [column(mean, first + q) for q in inside]
        for t in inside:
            k = first + t
            variance = jnp.full((SUB, LANES), variances[batch, k], jnp.float32)
            noise = variance * lax.rsqrt(variance)
            square = block[t, t]
            root = lax.rsqrt(square + (variance + SMALL_EPSILON))
            inverse = root * root
            below = 1.0 + noise * root
            guess = pl.reciprocal(below, approx=True)
            shrink = -inverse * (guess * (2.0 - below * guess))
            shift = (values[batch, k] - means[t]) * inverse
            row_own = spread(own[home], base + t)
            row_other = spread(other[home], base + t)
            seen_own = spread(lam_own[SUB * home:SUB * (home + 1)], base + t) * row_own
            seen_other = spread(lam_other[SUB * home:SUB * (home + 1)], base + t) * row_other
            hist_other[k:k + 1, :] = seen_other[:1]
            hist_rows[k:k + 1, :] = (shift * spin + shrink * row_own)[:1]
            mean = mean + shift * seen_own
            first_own = shrink * seen_own
            second_own = shrink * (row_own + square * first_own)
            first_other = shrink * seen_other
            second_other = shrink * (row_other + square * first_other)
            alpha, beta = {}, {}
            for q in range(t + 1, PANEL):
                linked = spread(lams[t][home], base + q) * block[t, q]
                alpha[q] = shrink * linked
                beta[q] = block[t, q] + square * alpha[q]
                means[q] = means[q] + shift * linked
            for a in range(t + 1, PANEL):
                for b in range(a, PANEL):
                    block[a, b] = (block[a, b] + alpha[b] * block[t, a]) + alpha[a] * beta[b]
            for i in live:
                g = cols[t][i]
                u = lams[t][i] * g
                scaled = shrink * u
                for q in range(t + 1, PANEL):
                    cols[q][i] = cols[q][i] + (g * alpha[q] + scaled * beta[q])
                own[i] = own[i] + (g * first_own + u * second_own)
                other[i] = other[i] + (g * first_other + u * second_other)


def filter_kernel(
    count, members, seen_ref, share_ref, geo_ref, geo_cols_ref, near_ref, chosen_ref, mine_ref,
    change_ref, hist_other, hist_rows, values, variances, sems,
):
    copies = [
        pltpu.make_async_copy(seen_ref.at[0], values, sems.at[0]),
        pltpu.make_async_copy(seen_ref.at[1], variances, sems.at[1]),
    ]
    for copy in copies:
        copy.start()
    picked = share_ref[:members, :]
    masks = share_ref[members:, :].astype(jnp.bfloat16)
    chosen = chosen_ref[...].astype(jnp.bfloat16)
    across = (((0,), (0,)), ((), ()))
    links = geo_ref[...] * lax.dot_general(masks, chosen, across, preferred_element_type=jnp.float32)
    lam_cols = geo_cols_ref[...] * lax.dot_general(chosen, masks, across, preferred_element_type=jnp.float32)
    mine = near_ref[...] * lax.dot_general(
        masks, mine_ref[...].astype(jnp.bfloat16), across, preferred_element_type=jnp.float32
    )
    left = lax.broadcasted_iota(jnp.int32, (count, LANES), 1) < count
    swapped = pltpu.roll(links, count, 1)
    eye = (
        lax.broadcasted_iota(jnp.int32, (members, members), 0)
        == lax.broadcasted_iota(jnp.int32, (members, members), 1)
    ).astype(jnp.float32)
    zeros = jnp.zeros((members, members), jnp.float32)

    spin = 1.0 / math.sqrt(members - 1.0)

    def begin(block):
        mean = jnp.sum(block, axis=0, keepdims=True) * (1.0 / members)
        return mean, (block - mean) * spin

    mean, apart = begin(picked)
    first, second = apart[:, :count], apart[:, count:]
    own = dot_rows(first, jnp.concatenate([first, eye], axis=1))
    other = dot_rows(first, jnp.concatenate([second * math.sqrt(members - 1.0), eye], axis=1))
    mean = jnp.broadcast_to(jnp.concatenate([mean[:, :count], mean[:, :count]], axis=1), (SUB, LANES))
    for copy in copies:
        copy.wait()
    batch_steps(
        values, variances, 0, count, own, other,
        jnp.where(left, links[:count], 0.0), jnp.where(left, swapped[:count], mine[:count]),
        lam_cols[:count], 0, mean, spin, hist_other, hist_rows,
    )
    moved = dot_rows(hist_rows[:, LANES - members:], hist_other[...])
    after = picked[:, count:] + moved[:, :count]
    change_one = moved[:, count:]

    mean, apart = begin(after)
    own = dot_rows(apart, jnp.concatenate([apart, eye], axis=1))
    other = jnp.concatenate([zeros, own[:, count:]], axis=1)
    mean = jnp.broadcast_to(jnp.concatenate([mean, mean], axis=1), (SUB, LANES))
    batch_steps(
        values, variances, 1, count, own, other,
        jnp.where(left, swapped[count:], 0.0), jnp.where(left, 0.0, mine[count:]),
        lam_cols[count:], count, mean, spin, hist_other, hist_rows,
    )
    change_two = dot_rows(hist_rows[:, LANES - members:], hist_other[:, LANES - members:])
    change_ref[...] = change_one + change_two + dot(change_two, change_one)


def apply_kernel(members, change_ref, mid_ref, core_ref, cross_ref, even_ref, odd_ref, out_hbm, out_ref, sems):
    change = change_ref[...]
    high = change.astype(jnp.bfloat16)
    low = (change - high.astype(jnp.float32)).astype(jnp.bfloat16)
    left = jnp.concatenate([high, high, low], axis=1)
    lane = lax.broadcasted_iota(jnp.int32, (SUB, LANES), 1)
    edge = jnp.logical_or(lane < STRIP, lane >= LANES - STRIP)
    even = (lane % (2 * STRIP) < STRIP) == (lax.rem(lax.axis_index("lon"), 2) == 0)

    def whole(field, row):
        main = mid_ref[field, row] + core_ref[field, row] + cross_ref[field, row]
        strip = jnp.where(even, even_ref[field, row], odd_ref[field, row])
        parts = []
        for group in range(members // SUB):
            turn = (2 * LANES - STRIP - 2 * STRIP * group) % LANES
            parts.append(jnp.where(edge, pltpu.roll(strip, turn, 1), 0.0))
        return main + jnp.concatenate(parts, axis=0)

    copies = [pltpu.make_async_copy(out_ref.at[field], out_hbm.at[field], sems.at[field]) for field in range(3)]
    for field in range(3):
        for row in range(0, SUB, 2):
            block = jnp.concatenate([whole(field, row), whole(field, row + 1)], axis=1)
            top = block.astype(jnp.bfloat16)
            rest = (block - top.astype(jnp.float32)).astype(jnp.bfloat16)
            right = jnp.concatenate([top, rest, top], axis=0)
            fresh = block + jnp.dot(left, right, preferred_element_type=jnp.float32)
            for extra in range(2):
                out_ref[field, pl.ds(row + extra, members, stride=SUB), :] = fresh[
                    :, extra * LANES:(extra + 1) * LANES
                ]
        copies[field].start()
    for copy in copies:
        copy.wait()


def closeness(lat_gap, lon_gap, total_cols):
    lon_gap = jnp.abs(lon_gap)
    lon_gap = jnp.minimum(lon_gap, total_cols - lon_gap)
    distance = (lat_gap * lat_gap + lon_gap * lon_gap).astype(jnp.float32)
    return 1.0 / (1.0 + distance / (LOC_RADIUS * LOC_RADIUS))


def body(model_variables, obs_cell, obs_value, obs_variance, tile_mask):
    members = model_variables.shape[1]
    rows_dev = model_variables.shape[2]
    cols_dev = model_variables.shape[3]
    count = obs_cell.shape[1]
    n_lat = lax.axis_size("lat")
    n_lon = lax.axis_size("lon")
    n_tiles = n_lat * n_lon
    lat = lax.axis_index("lat")
    lon = lax.axis_index("lon")
    total_cols = cols_dev * n_lon
    groups = members // SUB
    both = NBATCH * count
    vmem = pl.BlockSpec(memory_space=pltpu.VMEM)
    params = pltpu.CompilerParams(vmem_limit_bytes=VMEM_LIMIT)

    def array(*shape):
        return jax.ShapeDtypeStruct(shape, jnp.float32)

    wide = array(3, rows_dev, members, cols_dev)
    narrow = array(3, rows_dev, SUB, cols_dev)
    base = n_tiles // 4
    core_part, mid_part, cross_part, core_strip, mid_strip, cross_strip, share, seen_cell = pl.pallas_call(
        functools.partial(forecast_kernel, groups, members, n_lat, n_lon),
        out_shape=(wide,) * 3
        + (narrow,) * 3
        + (array(members + base, both), jax.ShapeDtypeStruct((NBATCH, count), jnp.int32)),
        in_specs=[pl.BlockSpec(memory_space=pl.ANY)] * 3,
        out_specs=(pl.BlockSpec(memory_space=pl.ANY),) * 3 + (vmem,) * 5,
        scratch_shapes=[
            pltpu.VMEM((3 * SUB, 2, members, LANES), jnp.float32),
            pltpu.SMEM((both + PICKS,), jnp.int32),
            pltpu.VMEM((3, 3 * SUB, SUB * JOINED, 2 * LANES), jnp.float32),
            pltpu.SMEM((NBATCH, count), jnp.int32),
            pltpu.VMEM((NBATCH, 1, count), jnp.int32),
            pltpu.VMEM((3, members * rows_dev, cols_dev), jnp.float32),
            pltpu.VMEM((3, 3, rows_dev, members, cols_dev), jnp.float32),
            pltpu.VMEM((3, rows_dev, SUB, cols_dev), jnp.float32),
            pltpu.VMEM((3, rows_dev, SUB, cols_dev), jnp.float32),
            pltpu.SemaphoreType.DMA((3,)),
            pltpu.SemaphoreType.DMA((groups // JOINED,)),
            pltpu.SemaphoreType.DMA((groups // JOINED, 3)),
        ],
        compiler_params=pltpu.CompilerParams(vmem_limit_bytes=FORECAST_LIMIT),
        name="forecast",
    )(
        obs_cell,
        jnp.swapaxes(tile_mask, 1, 2),
        model_variables.reshape(3, members * rows_dev, cols_dev),
    )

    def swap(x, axis, size, bit):
        return lax.ppermute(x, axis, [(i, i ^ (1 << bit)) for i in range(size)])

    def after(share, *others):
        return lax.optimization_barrier((share,) + others)

    core_pairs = [(i, i ^ 1) for i in range(n_lat)]
    cross_pairs = [p for i in range(1, n_lat - 1, 2) for p in ((i, i + 1), (i + 1, i))]
    even_pairs = [(i, i ^ 1) for i in range(n_lon)]
    odd_pairs = [p for i in range(1, n_lon, 2) for p in ((i, (i + 1) % n_lon), ((i + 1) % n_lon, i))]

    core_corner = lax.ppermute(core_strip, "lat", core_pairs)
    lat_bits = n_lat.bit_length() - 1
    lon_bits = n_lon.bit_length() - 1
    for bit in reversed(range(lat_bits)):
        share = share + swap(share, "lat", n_lat, bit)
        if bit == lat_bits - 1:
            share, cross_strip = after(share, cross_strip)
            cross_corner = lax.ppermute(cross_strip, "lat", cross_pairs)
    share, cross_part, obs_value, obs_variance = after(share, cross_part, obs_value, obs_variance)
    from_cross = lax.ppermute(cross_part, "lat", cross_pairs)
    seen = jnp.stack([obs_value, obs_variance])
    strips = mid_strip + core_corner + cross_corner
    for bit in range(lon_bits):
        if bit == lon_bits - 2:
            share, core_part = after(share, core_part)
            from_core = lax.ppermute(core_part, "lat", core_pairs)
        if bit == lon_bits - 1:
            share, strips = after(share, strips)
            from_even = lax.ppermute(strips, "lon", even_pairs)
            from_odd = lax.ppermute(strips, "lon", odd_pairs)
        other = swap(share, "lon", n_lon, bit)
        if bit < lon_bits - 2:
            share = share + other
        else:
            high = (lon >> bit) & 1
            mine, theirs = share[members:], other[members:]
            share = jnp.concatenate([
                share[:members] + other[:members],
                jnp.where(high == 1, theirs, mine),
                jnp.where(high == 1, mine, theirs),
            ])

    cells = seen_cell.reshape(both)
    obs_row = cells // total_cols
    obs_col = cells % total_cols
    home_lat = obs_row // rows_dev
    home_lon = obs_col // cols_dev
    centre_row = home_lat * rows_dev + rows_dev // 2
    centre_col = home_lon * cols_dev + cols_dev // 2
    geo = closeness(obs_row[:, None] - centre_row, obs_col[:, None] - centre_col, total_cols)
    geo_cols = closeness(obs_row - centre_row[:, None], obs_col - centre_col[:, None], total_cols)
    tiles = jnp.arange(n_tiles, dtype=jnp.int32)
    chosen = (tiles[:, None] == home_lon * n_lat + home_lat).astype(jnp.float32)
    near = closeness(
        obs_row - (lat * rows_dev + rows_dev // 2), obs_col - (lon * cols_dev + cols_dev // 2), total_cols
    )
    near = jnp.broadcast_to(near[:, None], (both, LANES))
    mine = jnp.broadcast_to((tiles == lon * n_lat + lat).astype(jnp.float32)[:, None], (n_tiles, LANES))

    change = pl.pallas_call(
        functools.partial(filter_kernel, count, members),
        out_shape=array(members, members),
        in_specs=[vmem] * 7,
        out_specs=vmem,
        scratch_shapes=[pltpu.VMEM((count, LANES), jnp.float32)] * 2
        + [pltpu.SMEM((NBATCH, count), jnp.float32)] * 2
        + [pltpu.SemaphoreType.DMA((2,))],
        compiler_params=params,
        name="filter",
    )(seen, share, geo, geo_cols, near, chosen, mine)

    out = pl.pallas_call(
        functools.partial(apply_kernel, members),
        out_shape=array(3, members * rows_dev, cols_dev),
        in_specs=[vmem] * 6,
        out_specs=pl.BlockSpec(memory_space=pl.ANY),
        scratch_shapes=[
            pltpu.VMEM((3, members * rows_dev, cols_dev), jnp.float32),
            pltpu.SemaphoreType.DMA((3,)),
        ],
        compiler_params=params,
        name="apply",
    )(change, mid_part, from_core, from_cross, from_even, from_odd)
    return out.reshape(3, members, rows_dev, cols_dev)


def solution(mesh):
    in_specs = (P(None, None, "lat", "lon"), P(), P(), P(), P(None, None, ("lon", "lat")))
    out_specs = P(None, None, "lat", "lon")
    return jax.shard_map(body, mesh=mesh, in_specs=in_specs, out_specs=out_specs, check_vma=False)
```

```python
import functools
import math

import jax
import jax.numpy as jnp
from jax import lax
from jax.experimental import pallas as pl
from jax.experimental.pallas import tpu as pltpu
from jax.sharding import PartitionSpec as P

STEPS = 4
NBATCH = 2
LOC_RADIUS = 256

CORIOLIS = 0.1
COURANT = 0.5
SMALL_EPSILON = 1e-06

SUB = 8
LANES = 128
STRIP = 8
PANEL = 8
PICKS = 4
HIGHEST = lax.Precision.HIGHEST
VMEM_LIMIT = 48 * 1024 * 1024
FORECAST_LIMIT = 53 * 1024 * 1024 + 320 * 1024


def dot(a, b):
    return jnp.dot(a, b, precision=HIGHEST, preferred_element_type=jnp.float32)


def dot_rows(a, b):
    return lax.dot_general(
        a, b, (((0,), (0,)), ((), ())), precision=HIGHEST, preferred_element_type=jnp.float32
    )


def forecast_kernel(
    groups, members, n_lat, n_lon, cell_hbm, mask_hbm, own_hbm,
    core_out, mid_out, cross_out, core_strip, mid_strip, cross_strip, share_ref, cell_out,
    slots, state, cell_ref, mask_ref, own_ref, small_sems, own_sems, out_sems,
):
    lat = lax.axis_index("lat")
    lon = lax.axis_index("lon")
    odd = lax.rem(lat, 2)
    total_rows = n_lat * SUB
    total_cols = n_lon * LANES
    lane = lax.broadcasted_iota(jnp.int32, (SUB, LANES), 1)
    zone = ((lane + STRIP) & (LANES - 1)) // (2 * STRIP)
    at_last = lane % (2 * STRIP) == 2 * STRIP - 1
    at_first = lane % (2 * STRIP) == 0
    scales, turns = [], []
    for row in range(-SUB, 2 * SUB):
        place = lat * SUB + row
        inside = jnp.logical_and(place >= 0, place < total_rows)
        spin = CORIOLIS * ((2.0 * place.astype(jnp.float32) + 1.0) / total_rows - 1.0)
        scales.append(jnp.where(inside, 0.5 * COURANT, 0.0))
        turns.append(jnp.where(inside, spin, 0.0))
    batches, count = cell_ref.shape
    own_copies = [
        pltpu.make_async_copy(own_hbm.at[field], own_ref.at[field], own_sems.at[field]) for field in (1, 2, 0)
    ]
    small = [
        pltpu.make_async_copy(source, target, small_sems.at[place])
        for place, (source, target) in enumerate((
            (cell_hbm, cell_ref), (cell_hbm, cell_out), (mask_hbm, mask_ref)
        ))
    ]
    for copy in own_copies + small:
        copy.start()

    def minus(a, b):
        if b is None:
            return a
        return -b if a is None else a - b

    def plus(a, b):
        if a is None or b is None:
            return b if a is None else a
        return a + b

    def times(scale, a):
        return None if a is None else scale * a

    def along(x):
        if x is None:
            return None
        right, left = pltpu.roll(x, LANES - 1, 1), pltpu.roll(x, 1, 1)
        rights = [right[SUB * g:SUB * (g + 1)] for g in range(groups + 1)]
        lefts = [left[SUB * g:SUB * (g + 1)] for g in range(groups + 1)]
        first, last = rights[0], lefts[0]
        for g in range(1, groups):
            first = jnp.where(zone == g, rights[g], first)
            last = jnp.where(zone == g, lefts[g], last)
        mend = jnp.where(at_last, rights[groups] - first, jnp.where(at_first, last - lefts[groups], 0.0))
        parts = [rights[g] - lefts[g] + jnp.where(zone == g, mend, 0.0) for g in range(groups)]
        parts.append(
            jnp.where(at_last, first, rights[groups]) - jnp.where(at_first, last, lefts[groups])
        )
        return jnp.concatenate(parts, axis=0)

    live = [dict() for _ in range(3)]

    def get(field, row):
        return state[field, row + SUB] if row in live[field] else None

    def put(field, row, value):
        if value is not None:
            live[field][row] = True
            state[field, row + SUB] = value

    def list_cells(start, stop, found):
        for index in range(start, stop):
            cell = cell_ref[index // count, index % count]
            row = lax.div(cell, total_cols)
            col = cell - row * total_cols - lon * LANES
            row = row - lat * SUB + SUB
            col = jnp.where(col < 0, col + total_cols, col)
            west = col >= total_cols - STRIP
            near = jnp.logical_and(row > 0, row < 3 * SUB - 1)
            near = jnp.logical_and(near, jnp.logical_or(col < LANES + STRIP, west))
            ring = jnp.where(west, col + (2 * LANES - total_cols), col)
            slots[found] = (row * (2 * LANES) + ring) * LANES + index
            found = found + near.astype(jnp.int32)
        return found

    for copy in small:
        copy.wait()
    for field, copy in zip((1, 2, 0), own_copies):
        copy.wait()
        for row in range(SUB):
            pieces = [
                own_ref[field, pl.ds(group * SUB * SUB + row, SUB, stride=SUB), :] for group in range(groups)
            ]
            pieces = [pieces[0]] + [pltpu.roll(pieces[g], 2 * STRIP * g, 1) for g in range(1, groups)]
            put(field, row, jnp.concatenate(pieces + [jnp.zeros((SUB, LANES), jnp.float32)], axis=0))

    cells = batches * count
    part_rows = [2 * SUB - 2 * SUB * odd, SUB, 2 * SUB * odd]
    outs = [core_out, mid_out, cross_out]

    def out_copy(part, fields):
        rows = pl.ds(part_rows[part], SUB)
        return pltpu.make_async_copy(
            state.at[fields, rows, pl.ds(0, members)], outs[part].at[fields],
            out_sems.at[part, 0 if fields.size == 1 else 1],
        )

    for row in (-SUB, 2 * SUB - 1):
        for field in range(2):
            state[field, row + SUB] = jnp.zeros((members + SUB, LANES), jnp.float32)
    found = jnp.int32(0)
    for step in range(STEPS):
        for row in range(-SUB, 2 * SUB):
            slope = plus(along(get(1, row)), minus(get(2, row + 1), get(2, row - 1)))
            put(0, row, minus(get(0, row), times(scales[row + SUB], slope)))
        found = list_cells(cells * step // STEPS, cells * (step + 1) // STEPS, found)
        if step == STEPS - 1:
            for part in range(3):
                out_copy(part, pl.ds(0, 1)).start()
        for row in range(-SUB, 2 * SUB):
            east, north = get(1, row), get(2, row)
            slope = minus(get(0, row + 1), get(0, row - 1))
            put(1, row, minus(plus(east, times(turns[row + SUB], north)), times(scales[row + SUB], along(get(0, row)))))
            put(2, row, minus(minus(north, times(turns[row + SUB], east)), times(scales[row + SUB], slope)))
    for part in range(3):
        out_copy(part, pl.ds(1, 2)).start()

    halo = pl.ds(members, SUB)
    for field in range(3):
        up, down = state[field, pl.ds(0, SUB), halo, :], state[field, pl.ds(2 * SUB, SUB), halo, :]
        mid_strip[field] = state[field, pl.ds(SUB, SUB), halo, :]
        core_strip[field] = jnp.where(odd == 1, up, down)
        cross_strip[field] = jnp.where(odd == 1, down, up)
    tiles = share_ref.shape[0] - members
    mine = lax.broadcasted_iota(jnp.int32, (tiles, LANES), 0) == lax.rem(lon * n_lat + lat, tiles)
    mask = jnp.concatenate([mask_ref[batch] for batch in range(batches)], axis=1).astype(jnp.float32)
    share_ref[members:, :] = jnp.where(mine, mask, 0.0)
    wide = lax.broadcasted_iota(jnp.int32, (members, LANES), 1)

    def pick(turn, share):
        for extra in range(PICKS):
            item = turn * PICKS + extra
            packed = jnp.where(item < found, slots[item], 0)
            index = packed & (LANES - 1)
            ring = (packed >> 7) & (2 * LANES - 1)
            row = packed >> 15
            pieces = []
            for group in range(groups):
                place = pl.multiple_of(jnp.where(ring < LANES, group * SUB, members), SUB)
                piece = state[0, row, pl.ds(place, SUB), :]
                pieces.append(pltpu.roll(piece, (index - ring - 2 * STRIP * group) & (LANES - 1), 1))
            turned = jnp.concatenate(pieces, axis=0)
            share = jnp.where(wide == jnp.where(item < found, index, LANES), turned, share)
        return share

    share_ref[:members, :] = lax.fori_loop(
        0, lax.div(found + PICKS - 1, PICKS), pick, jnp.zeros((members, LANES), jnp.float32)
    )
    for part in range(3):
        out_copy(part, pl.ds(0, 1)).wait()
        out_copy(part, pl.ds(1, 2)).wait()


def batch_steps(
    values, variances, batch, count, own, other, lam_own, lam_other, lam_cols, offset, mean, spin,
    hist_other, hist_rows, lam_rows, spare,
):
    groups = count // SUB
    own = [own[SUB * i:SUB * (i + 1)] for i in range(groups)]
    other = [other[SUB * i:SUB * (i + 1)] for i in range(groups)]

    lam_rows[batch, 0] = lam_own
    lam_rows[batch, 1] = lam_other

    def lam_row(side, k):
        return jnp.broadcast_to(lam_rows[batch, side, k:k + 1, :], (SUB, LANES))

    def column(x, lane):
        return jnp.broadcast_to(x[:, lane:lane + 1], (SUB, LANES))

    for first in range(0, count, PANEL):
        home, base = divmod(first, SUB)
        live = range(home, groups)
        inside = range(PANEL)
        cols = [{i: column(own[i], first + q) for i in live} for q in inside]
        lams = [
            {i: column(lam_cols[SUB * i:SUB * (i + 1)], offset + first + q) for i in live} for q in inside
        ]
        place = batch * groups + home

        def keep(slot, x):
            spare[place, slot] = x

        def spread(slot, row):
            return jnp.broadcast_to(spare[place, slot, row:row + 1, :], (SUB, LANES))

        for q in inside:
            keep(q, cols[q][home])
        keep(2 * PANEL, own[home])
        keep(2 * PANEL + 1, other[home])
        for q in inside:
            keep(PANEL + q, lams[q][home])
        block = {(a, b): spread(b, base + a) for a in inside for b in inside if a <= b}
        rows_own = [spread(2 * PANEL, base + q) for q in inside]
        rows_other = [spread(2 * PANEL + 1, base + q) for q in inside]
        means = [column(mean, first + q) for q in inside]
        noises = [jnp.full((SUB, LANES), variances[batch, first + q], jnp.float32) for q in inside]
        total = block[0, 0] + (noises[0] + SMALL_EPSILON)
        for t in inside:
            k = first + t
            noise = noises[t] * lax.rsqrt(noises[t])
            square = block[t, t]
            root = lax.rsqrt(total)
            inverse = root * root
            below = 1.0 + noise * root
            guess = pl.reciprocal(below, approx=True)
            shrink = (inverse * guess) * (below * guess - 2.0)
            shift = (values[batch, k] - means[t]) * inverse
            row_own, row_other = rows_own[t], rows_other[t]
            seen_own = lam_row(0, k) * row_own
            seen_other = lam_row(1, k) * row_other
            hist_other[k:k + 1, :] = seen_other[:1]
            hist_rows[k:k + 1, :] = (shift * spin + shrink * row_own)[:1]
            mean = mean + shift * seen_own
            first_own = shrink * seen_own
            second_own = shrink * (row_own + square * first_own)
            first_other = shrink * seen_other
            second_other = shrink * (row_other + square * first_other)
            alpha, beta = {}, {}
            if t + 1 < PANEL:
                linked = spread(PANEL + t, base + t + 1) * block[t, t + 1]
                flat = block[t + 1, t + 1] + (noises[t + 1] + SMALL_EPSILON)
                total = flat + shrink * (2.0 * (linked * block[t, t + 1]) + shrink * (linked * linked * square))
            for q in range(t + 1, PANEL):
                linked = spread(PANEL + t, base + q) * block[t, q]
                alpha[q] = shrink * linked
                beta[q] = block[t, q] + square * alpha[q]
                rows_own[q] = rows_own[q] + (block[t, q] * first_own + linked * second_own)
                rows_other[q] = rows_other[q] + (block[t, q] * first_other + linked * second_other)
                means[q] = means[q] + shift * linked
            for a in range(t + 1, PANEL):
                for b in range(a, PANEL):
                    block[a, b] = (block[a, b] + alpha[b] * block[t, a]) + alpha[a] * beta[b]
            for i in live[1:]:
                g = cols[t][i]
                u = lams[t][i] * g
                scaled = shrink * u
                for q in range(t + 1, PANEL):
                    cols[q][i] = cols[q][i] + (g * alpha[q] + scaled * beta[q])
                own[i] = own[i] + (g * first_own + u * second_own)
                other[i] = other[i] + (g * first_other + u * second_other)


def filter_kernel(
    count, members, seen_ref, share_ref, geo_ref, geo_cols_ref, near_ref, chosen_ref, mine_ref,
    change_ref, hist_other, hist_rows, lam_rows, spare, values, variances, sems,
):
    copies = [
        pltpu.make_async_copy(seen_ref.at[0], values, sems.at[0]),
        pltpu.make_async_copy(seen_ref.at[1], variances, sems.at[1]),
    ]
    for copy in copies:
        copy.start()
    picked = share_ref[:members, :]
    masks = share_ref[members:, :].astype(jnp.bfloat16)
    chosen = chosen_ref[...].astype(jnp.bfloat16)
    across = (((0,), (0,)), ((), ()))
    links = geo_ref[...] * lax.dot_general(masks, chosen, across, preferred_element_type=jnp.float32)
    lam_cols = geo_cols_ref[...] * lax.dot_general(chosen, masks, across, preferred_element_type=jnp.float32)
    mine = near_ref[...] * lax.dot_general(
        masks, mine_ref[...].astype(jnp.bfloat16), across, preferred_element_type=jnp.float32
    )
    left = lax.broadcasted_iota(jnp.int32, (count, LANES), 1) < count
    swapped = pltpu.roll(links, count, 1)
    eye = (
        lax.broadcasted_iota(jnp.int32, (members, members), 0)
        == lax.broadcasted_iota(jnp.int32, (members, members), 1)
    ).astype(jnp.float32)
    zeros = jnp.zeros((members, members), jnp.float32)

    spin = 1.0 / math.sqrt(members - 1.0)

    def begin(block):
        mean = jnp.sum(block, axis=0, keepdims=True) * (1.0 / members)
        return mean, (block - mean) * spin

    mean, apart = begin(picked)
    first, second = apart[:, :count], apart[:, count:]
    own = dot_rows(first, jnp.concatenate([first, eye], axis=1))
    other = dot_rows(first, jnp.concatenate([second * math.sqrt(members - 1.0), eye], axis=1))
    mean = jnp.broadcast_to(jnp.concatenate([mean[:, :count], mean[:, :count]], axis=1), (SUB, LANES))
    for copy in copies:
        copy.wait()
    batch_steps(
        values, variances, 0, count, own, other,
        jnp.where(left, links[:count], 0.0), jnp.where(left, swapped[:count], mine[:count]),
        lam_cols[:count], 0, mean, spin, hist_other, hist_rows, lam_rows, spare,
    )
    moved = dot_rows(hist_rows[:, LANES - members:], hist_other[...])
    after = picked[:, count:] + moved[:, :count]
    change_one = moved[:, count:]

    mean, apart = begin(after)
    own = dot_rows(apart, jnp.concatenate([apart, eye], axis=1))
    other = jnp.concatenate([zeros, own[:, count:]], axis=1)
    mean = jnp.broadcast_to(jnp.concatenate([mean, mean], axis=1), (SUB, LANES))
    batch_steps(
        values, variances, 1, count, own, other,
        jnp.where(left, swapped[count:], 0.0), jnp.where(left, 0.0, mine[count:]),
        lam_cols[count:], count, mean, spin, hist_other, hist_rows, lam_rows, spare,
    )
    change_two = dot_rows(hist_rows[:, LANES - members:], hist_other[:, LANES - members:])
    change_ref[...] = change_one + change_two + dot(change_two, change_one)


def apply_kernel(members, change_ref, mid_ref, core_ref, cross_ref, even_ref, odd_ref, out_hbm, out_ref, sems):
    change = change_ref[...]
    high = change.astype(jnp.bfloat16)
    low = (change - high.astype(jnp.float32)).astype(jnp.bfloat16)
    left = jnp.concatenate([high, high, low], axis=1)
    lane = lax.broadcasted_iota(jnp.int32, (SUB, LANES), 1)
    zone = ((lane + STRIP) & (LANES - 1)) // (2 * STRIP)
    even = (lane % (2 * STRIP) >= STRIP) == (lax.rem(lax.axis_index("lon"), 2) == 0)

    def whole(field, row):
        main = mid_ref[field, row] + core_ref[field, row] + cross_ref[field, row]
        strip = jnp.where(even, even_ref[field, row], odd_ref[field, row])
        parts = []
        for group in range(members // SUB):
            part = main[SUB * group:SUB * (group + 1)] + jnp.where(zone == group, strip, 0.0)
            parts.append(pltpu.roll(part, LANES - 2 * STRIP * group, 1) if group else part)
        return jnp.concatenate(parts, axis=0)

    copies = [pltpu.make_async_copy(out_ref.at[field], out_hbm.at[field], sems.at[field]) for field in range(3)]
    for field in range(3):
        for row in range(0, SUB, 2):
            block = jnp.concatenate([whole(field, row), whole(field, row + 1)], axis=1)
            top = block.astype(jnp.bfloat16)
            rest = (block - top.astype(jnp.float32)).astype(jnp.bfloat16)
            right = jnp.concatenate([top, rest, top], axis=0)
            fresh = block + jnp.dot(left, right, preferred_element_type=jnp.float32)
            for extra in range(2):
                out_ref[field, pl.ds(row + extra, members, stride=SUB), :] = fresh[
                    :, extra * LANES:(extra + 1) * LANES
                ]
        copies[field].start()
    for copy in copies:
        copy.wait()


def closeness(lat_gap, lon_gap, total_cols):
    lon_gap = jnp.abs(lon_gap)
    lon_gap = jnp.minimum(lon_gap, total_cols - lon_gap)
    distance = (lat_gap * lat_gap + lon_gap * lon_gap).astype(jnp.float32)
    return 1.0 / (1.0 + distance / (LOC_RADIUS * LOC_RADIUS))


def body(model_variables, obs_cell, obs_value, obs_variance, tile_mask):
    members = model_variables.shape[1]
    rows_dev = model_variables.shape[2]
    cols_dev = model_variables.shape[3]
    count = obs_cell.shape[1]
    n_lat = lax.axis_size("lat")
    n_lon = lax.axis_size("lon")
    n_tiles = n_lat * n_lon
    lat = lax.axis_index("lat")
    lon = lax.axis_index("lon")
    total_cols = cols_dev * n_lon
    groups = members // SUB
    both = NBATCH * count
    vmem = pl.BlockSpec(memory_space=pltpu.VMEM)
    params = pltpu.CompilerParams(vmem_limit_bytes=VMEM_LIMIT)

    def array(*shape):
        return jax.ShapeDtypeStruct(shape, jnp.float32)

    wide = array(3, rows_dev, members, cols_dev)
    narrow = array(3, rows_dev, SUB, cols_dev)
    base = n_tiles // 4
    core_part, mid_part, cross_part, core_strip, mid_strip, cross_strip, share, seen_cell = pl.pallas_call(
        functools.partial(forecast_kernel, groups, members, n_lat, n_lon),
        out_shape=(wide,) * 3
        + (narrow,) * 3
        + (array(members + base, both), jax.ShapeDtypeStruct((NBATCH, count), jnp.int32)),
        in_specs=[pl.BlockSpec(memory_space=pl.ANY)] * 3,
        out_specs=(pl.BlockSpec(memory_space=pl.ANY),) * 3 + (vmem,) * 5,
        scratch_shapes=[
            pltpu.SMEM((both + PICKS,), jnp.int32),
            pltpu.VMEM((3, 3 * SUB, members + SUB, LANES), jnp.float32),
            pltpu.SMEM((NBATCH, count), jnp.int32),
            pltpu.VMEM((NBATCH, 1, count), jnp.int32),
            pltpu.VMEM((3, members * rows_dev, cols_dev), jnp.float32),
            pltpu.SemaphoreType.DMA((3,)),
            pltpu.SemaphoreType.DMA((3,)),
            pltpu.SemaphoreType.DMA((3, 2)),
        ],
        compiler_params=pltpu.CompilerParams(vmem_limit_bytes=FORECAST_LIMIT),
        name="forecast",
    )(
        obs_cell,
        jnp.swapaxes(tile_mask, 1, 2),
        model_variables.reshape(3, members * rows_dev, cols_dev),
    )

    def swap(x, axis, size, bit):
        return lax.ppermute(x, axis, [(i, i ^ (1 << bit)) for i in range(size)])

    def after(share, *others):
        return lax.optimization_barrier((share,) + others)

    core_pairs = [(i, i ^ 1) for i in range(n_lat)]
    cross_pairs = [p for i in range(1, n_lat - 1, 2) for p in ((i, i + 1), (i + 1, i))]
    even_pairs = [(i, i ^ 1) for i in range(n_lon)]
    odd_pairs = [p for i in range(1, n_lon, 2) for p in ((i, (i + 1) % n_lon), ((i + 1) % n_lon, i))]

    cross_corner = lax.ppermute(cross_strip, "lat", cross_pairs)
    lat_bits = n_lat.bit_length() - 1
    lon_bits = n_lon.bit_length() - 1
    for bit in reversed(range(1, lat_bits)):
        share = share + swap(share, "lat", n_lat, bit)
    corner_rows = core_strip.size // both
    message = jnp.concatenate([share, core_strip.reshape(corner_rows, both)])
    message = lax.ppermute(message, "lat", core_pairs)
    share = share + message[:share.shape[0]]
    core_corner = message[share.shape[0]:].reshape(core_strip.shape)
    share, cross_part, obs_value, obs_variance = after(share, cross_part, obs_value, obs_variance)
    from_cross = lax.ppermute(cross_part, "lat", cross_pairs)
    seen = jnp.stack([obs_value, obs_variance])
    strips = mid_strip + core_corner + cross_corner
    for bit in range(lon_bits):
        if bit == lon_bits - 2:
            share, core_part, seen = after(share, core_part, seen)
            from_core = lax.ppermute(core_part, "lat", core_pairs)
        if bit == lon_bits - 1:
            share, strips = after(share, strips)
            from_even = lax.ppermute(strips, "lon", even_pairs)
            from_odd = lax.ppermute(strips, "lon", odd_pairs)
        other = swap(share, "lon", n_lon, bit)
        if bit < lon_bits - 2:
            share = share + other
        else:
            high = (lon >> bit) & 1
            mine, theirs = share[members:], other[members:]
            share = jnp.concatenate([
                share[:members] + other[:members],
                jnp.where(high == 1, theirs, mine),
                jnp.where(high == 1, mine, theirs),
            ])

    cells = seen_cell.reshape(both)
    obs_row = cells // total_cols
    obs_col = cells % total_cols
    home_lat = obs_row // rows_dev
    home_lon = obs_col // cols_dev
    centre_row = home_lat * rows_dev + rows_dev // 2
    centre_col = home_lon * cols_dev + cols_dev // 2
    geo = closeness(obs_row[:, None] - centre_row, obs_col[:, None] - centre_col, total_cols)
    geo_cols = closeness(obs_row - centre_row[:, None], obs_col - centre_col[:, None], total_cols)
    tiles = jnp.arange(n_tiles, dtype=jnp.int32)
    chosen = (tiles[:, None] == home_lon * n_lat + home_lat).astype(jnp.float32)
    near = closeness(
        obs_row - (lat * rows_dev + rows_dev // 2), obs_col - (lon * cols_dev + cols_dev // 2), total_cols
    )
    near = jnp.broadcast_to(near[:, None], (both, LANES))
    mine = jnp.broadcast_to((tiles == lon * n_lat + lat).astype(jnp.float32)[:, None], (n_tiles, LANES))

    change = pl.pallas_call(
        functools.partial(filter_kernel, count, members),
        out_shape=array(members, members),
        in_specs=[vmem] * 7,
        out_specs=vmem,
        scratch_shapes=[pltpu.VMEM((count, LANES), jnp.float32)] * 2
        + [
            pltpu.VMEM((NBATCH, 2, count, LANES), jnp.float32),
            pltpu.VMEM((NBATCH * count // SUB, 2 * PANEL + 2, SUB, LANES), jnp.float32),
        ]
        + [pltpu.SMEM((NBATCH, count), jnp.float32)] * 2
        + [pltpu.SemaphoreType.DMA((2,))],
        compiler_params=params,
        name="filter",
    )(seen, share, geo, geo_cols, near, chosen, mine)

    out = pl.pallas_call(
        functools.partial(apply_kernel, members),
        out_shape=array(3, members * rows_dev, cols_dev),
        in_specs=[vmem] * 6,
        out_specs=pl.BlockSpec(memory_space=pl.ANY),
        scratch_shapes=[
            pltpu.VMEM((3, members * rows_dev, cols_dev), jnp.float32),
            pltpu.SemaphoreType.DMA((3,)),
        ],
        compiler_params=params,
        name="apply",
    )(change, mid_part, from_core, from_cross, from_even, from_odd)
    return out.reshape(3, members, rows_dev, cols_dev)


def solution(mesh):
    in_specs = (P(None, None, "lat", "lon"), P(), P(), P(), P(None, None, ("lon", "lat")))
    out_specs = P(None, None, "lat", "lon")
    return jax.shard_map(body, mesh=mesh, in_specs=in_specs, out_specs=out_specs, check_vma=False)
```

```python
import functools
import math

import jax
import jax.numpy as jnp
from jax import lax
from jax.experimental import pallas as pl
from jax.experimental.pallas import tpu as pltpu
from jax.sharding import PartitionSpec as P

STEPS = 4
NBATCH = 2
LOC_RADIUS = 256

CORIOLIS = 0.1
COURANT = 0.5
SMALL_EPSILON = 1e-06

SUB = 8
LANES = 128
STRIP = 8
PANEL = 8
PICKS = 4
HIGHEST = lax.Precision.HIGHEST
VMEM_LIMIT = 48 * 1024 * 1024
FORECAST_LIMIT = 53 * 1024 * 1024 + 320 * 1024


def dot(a, b):
    return jnp.dot(a, b, precision=HIGHEST, preferred_element_type=jnp.float32)


def dot_rows(a, b):
    return lax.dot_general(
        a, b, (((0,), (0,)), ((), ())), precision=HIGHEST, preferred_element_type=jnp.float32
    )


def forecast_kernel(
    groups, members, n_lat, n_lon, cell_hbm, mask_hbm, own_hbm,
    core_out, mid_out, cross_out, core_strip, mid_strip, cross_strip, share_ref, cell_out,
    slots, state, cell_ref, mask_ref, own_ref, small_sems, own_sems, out_sems,
):
    lat = lax.axis_index("lat")
    lon = lax.axis_index("lon")
    odd = lax.rem(lat, 2)
    total_rows = n_lat * SUB
    total_cols = n_lon * LANES
    lane = lax.broadcasted_iota(jnp.int32, (SUB, LANES), 1)
    zone = ((lane + STRIP) & (LANES - 1)) // (2 * STRIP)
    at_last = lane % (2 * STRIP) == 2 * STRIP - 1
    at_first = lane % (2 * STRIP) == 0
    scales, turns = [], []
    for row in range(-SUB, 2 * SUB):
        place = lat * SUB + row
        inside = jnp.logical_and(place >= 0, place < total_rows)
        spin = CORIOLIS * ((2.0 * place.astype(jnp.float32) + 1.0) / total_rows - 1.0)
        scales.append(jnp.where(inside, 0.5 * COURANT, 0.0))
        turns.append(jnp.where(inside, spin, 0.0))
    batches, count = cell_ref.shape
    own_copies = [
        pltpu.make_async_copy(own_hbm.at[field], own_ref.at[field], own_sems.at[field]) for field in (1, 2, 0)
    ]
    small = [
        pltpu.make_async_copy(source, target, small_sems.at[place])
        for place, (source, target) in enumerate((
            (cell_hbm, cell_ref), (cell_hbm, cell_out), (mask_hbm, mask_ref)
        ))
    ]
    for copy in own_copies + small:
        copy.start()

    def minus(a, b):
        if b is None:
            return a
        return -b if a is None else a - b

    def plus(a, b):
        if a is None or b is None:
            return b if a is None else a
        return a + b

    def times(scale, a):
        return None if a is None else scale * a

    def along(x):
        if x is None:
            return None
        right, left = pltpu.roll(x, LANES - 1, 1), pltpu.roll(x, 1, 1)
        rights = [right[SUB * g:SUB * (g + 1)] for g in range(groups + 1)]
        lefts = [left[SUB * g:SUB * (g + 1)] for g in range(groups + 1)]
        first, last = rights[0], lefts[0]
        for g in range(1, groups):
            first = jnp.where(zone == g, rights[g], first)
            last = jnp.where(zone == g, lefts[g], last)
        mend = jnp.where(at_last, rights[groups] - first, jnp.where(at_first, last - lefts[groups], 0.0))
        parts = [rights[g] - lefts[g] + jnp.where(zone == g, mend, 0.0) for g in range(groups)]
        parts.append(
            jnp.where(at_last, first, rights[groups]) - jnp.where(at_first, last, lefts[groups])
        )
        return jnp.concatenate(parts, axis=0)

    live = [dict() for _ in range(3)]

    def get(field, row):
        return state[field, row + SUB] if row in live[field] else None

    def put(field, row, value):
        if value is not None:
            live[field][row] = True
            state[field, row + SUB] = value

    def list_cells(start, stop, found):
        for index in range(start, stop):
            cell = cell_ref[index // count, index % count]
            row = lax.div(cell, total_cols)
            col = cell - row * total_cols - lon * LANES
            row = row - lat * SUB + SUB
            col = jnp.where(col < 0, col + total_cols, col)
            west = col >= total_cols - STRIP
            near = jnp.logical_and(row > 0, row < 3 * SUB - 1)
            near = jnp.logical_and(near, jnp.logical_or(col < LANES + STRIP, west))
            ring = jnp.where(west, col + (2 * LANES - total_cols), col)
            slots[found] = (row * (2 * LANES) + ring) * LANES + index
            found = found + near.astype(jnp.int32)
        return found

    for copy in small:
        copy.wait()
    for field, copy in zip((1, 2, 0), own_copies):
        copy.wait()
        for row in range(SUB):
            pieces = [
                own_ref[field, pl.ds(group * SUB * SUB + row, SUB, stride=SUB), :] for group in range(groups)
            ]
            pieces = [pieces[0]] + [pltpu.roll(pieces[g], 2 * STRIP * g, 1) for g in range(1, groups)]
            put(field, row, jnp.concatenate(pieces + [jnp.zeros((SUB, LANES), jnp.float32)], axis=0))

    cells = batches * count
    part_rows = [2 * SUB - 2 * SUB * odd, SUB, 2 * SUB * odd]
    outs = [core_out, mid_out, cross_out]

    def out_copy(part, fields):
        rows = pl.ds(part_rows[part], SUB)
        return pltpu.make_async_copy(
            state.at[fields, rows, pl.ds(0, members)], outs[part].at[fields],
            out_sems.at[part, 0 if fields.size == 1 else 1],
        )

    for row in (-SUB, 2 * SUB - 1):
        for field in range(2):
            state[field, row + SUB] = jnp.zeros((members + SUB, LANES), jnp.float32)
    found = jnp.int32(0)
    for step in range(STEPS):
        for row in range(-SUB, 2 * SUB):
            slope = plus(along(get(1, row)), minus(get(2, row + 1), get(2, row - 1)))
            put(0, row, minus(get(0, row), times(scales[row + SUB], slope)))
        found = list_cells(cells * step // STEPS, cells * (step + 1) // STEPS, found)
        if step == STEPS - 1:
            for part in range(3):
                out_copy(part, pl.ds(0, 1)).start()
        for row in range(-SUB, 2 * SUB):
            east, north = get(1, row), get(2, row)
            slope = minus(get(0, row + 1), get(0, row - 1))
            put(1, row, minus(plus(east, times(turns[row + SUB], north)), times(scales[row + SUB], along(get(0, row)))))
            put(2, row, minus(minus(north, times(turns[row + SUB], east)), times(scales[row + SUB], slope)))
    for part in range(3):
        out_copy(part, pl.ds(1, 2)).start()

    halo = pl.ds(members, SUB)
    for field in range(3):
        up, down = state[field, pl.ds(0, SUB), halo, :], state[field, pl.ds(2 * SUB, SUB), halo, :]
        mid_strip[field] = state[field, pl.ds(SUB, SUB), halo, :]
        core_strip[field] = jnp.where(odd == 1, up, down)
        cross_strip[field] = jnp.where(odd == 1, down, up)
    tiles = share_ref.shape[0] - members
    mine = lax.broadcasted_iota(jnp.int32, (tiles, LANES), 0) == lax.rem(lon * n_lat + lat, tiles)
    mask = jnp.concatenate([mask_ref[batch] for batch in range(batches)], axis=1).astype(jnp.float32)
    share_ref[members:, :] = jnp.where(mine, mask, 0.0)
    wide = lax.broadcasted_iota(jnp.int32, (members, LANES), 1)

    def pick(turn, share):
        for extra in range(PICKS):
            item = turn * PICKS + extra
            packed = jnp.where(item < found, slots[item], 0)
            index = packed & (LANES - 1)
            ring = (packed >> 7) & (2 * LANES - 1)
            row = packed >> 15
            pieces = []
            for group in range(groups):
                place = pl.multiple_of(jnp.where(ring < LANES, group * SUB, members), SUB)
                piece = state[0, row, pl.ds(place, SUB), :]
                pieces.append(pltpu.roll(piece, (index - ring - 2 * STRIP * group) & (LANES - 1), 1))
            turned = jnp.concatenate(pieces, axis=0)
            share = jnp.where(wide == jnp.where(item < found, index, LANES), turned, share)
        return share

    share_ref[:members, :] = lax.fori_loop(
        0, lax.div(found + PICKS - 1, PICKS), pick, jnp.zeros((members, LANES), jnp.float32)
    )
    for part in range(3):
        out_copy(part, pl.ds(0, 1)).wait()
        out_copy(part, pl.ds(1, 2)).wait()


def batch_steps(
    values, variances, batch, count, own, other, lam_own, lam_other, lam_cols, offset, mean, spin,
    hist_other, hist_rows, lam_rows, spare,
):
    groups = count // SUB
    own = [own[SUB * i:SUB * (i + 1)] for i in range(groups)]
    other = [other[SUB * i:SUB * (i + 1)] for i in range(groups)]

    lam_rows[batch, 0] = lam_own
    lam_rows[batch, 1] = lam_other

    def lam_row(side, k):
        return jnp.broadcast_to(lam_rows[batch, side, k:k + 1, :], (SUB, LANES))

    def column(x, lane):
        return jnp.broadcast_to(x[:, lane:lane + 1], (SUB, LANES))

    for first in range(0, count, PANEL):
        home, base = divmod(first, SUB)
        live = range(home, groups)
        inside = range(PANEL)
        cols = [{i: column(own[i], first + q) for i in live} for q in inside]
        lams = [
            {i: column(lam_cols[SUB * i:SUB * (i + 1)], offset + first + q) for i in live} for q in inside
        ]
        place = batch * groups + home

        def keep(slot, x):
            spare[place, slot] = x

        def spread(slot, row):
            return jnp.broadcast_to(spare[place, slot, row:row + 1, :], (SUB, LANES))

        for q in inside:
            keep(q, cols[q][home])
        keep(2 * PANEL, own[home])
        keep(2 * PANEL + 1, other[home])
        for q in inside:
            keep(PANEL + q, lams[q][home])
        block = {(a, b): spread(b, base + a) for a in inside for b in inside if a <= b}
        rows_own = [spread(2 * PANEL, base + q) for q in inside]
        rows_other = [spread(2 * PANEL + 1, base + q) for q in inside]
        means = [column(mean, first + q) for q in inside]
        noises = [jnp.full((SUB, LANES), variances[batch, first + q], jnp.float32) for q in inside]
        total = block[0, 0] + (noises[0] + SMALL_EPSILON)
        for t in inside:
            k = first + t
            noise = noises[t] * lax.rsqrt(noises[t])
            square = block[t, t]
            root = lax.rsqrt(total)
            inverse = root * root
            below = 1.0 + noise * root
            guess = pl.reciprocal(below, approx=True)
            shrink = (inverse * guess) * (below * guess - 2.0)
            shift = (values[batch, k] - means[t]) * inverse
            row_own, row_other = rows_own[t], rows_other[t]
            seen_own = lam_row(0, k) * row_own
            seen_other = lam_row(1, k) * row_other
            hist_other[k:k + 1, :] = seen_other[:1]
            hist_rows[k:k + 1, :] = (shift * spin + shrink * row_own)[:1]
            mean = mean + shift * seen_own
            first_own = shrink * seen_own
            second_own = shrink * (row_own + square * first_own)
            first_other = shrink * seen_other
            second_other = shrink * (row_other + square * first_other)
            alpha, beta = {}, {}
            if t + 1 < PANEL:
                linked = spread(PANEL + t, base + t + 1) * block[t, t + 1]
                flat = block[t + 1, t + 1] + (noises[t + 1] + SMALL_EPSILON)
                total = flat + shrink * (2.0 * (linked * block[t, t + 1]) + shrink * (linked * linked * square))
            for q in range(t + 1, PANEL):
                linked = spread(PANEL + t, base + q) * block[t, q]
                alpha[q] = shrink * linked
                beta[q] = block[t, q] + square * alpha[q]
                rows_own[q] = rows_own[q] + (block[t, q] * first_own + linked * second_own)
                rows_other[q] = rows_other[q] + (block[t, q] * first_other + linked * second_other)
                means[q] = means[q] + shift * linked
            for a in range(t + 1, PANEL):
                for b in range(a, PANEL):
                    block[a, b] = (block[a, b] + alpha[b] * block[t, a]) + alpha[a] * beta[b]
            for i in live[1:]:
                g = cols[t][i]
                u = lams[t][i] * g
                scaled = shrink * u
                for q in range(t + 1, PANEL):
                    cols[q][i] = cols[q][i] + (g * alpha[q] + scaled * beta[q])
                own[i] = own[i] + (g * first_own + u * second_own)
                other[i] = other[i] + (g * first_other + u * second_other)


def filter_kernel(
    count, members, seen_ref, share_ref, geo_ref, geo_cols_ref, near_ref, chosen_ref, mine_ref,
    change_ref, hist_other, hist_rows, lam_rows, spare, values, variances, sems,
):
    copies = [
        pltpu.make_async_copy(seen_ref.at[0], values, sems.at[0]),
        pltpu.make_async_copy(seen_ref.at[1], variances, sems.at[1]),
    ]
    for copy in copies:
        copy.start()
    picked = share_ref[:members, :]
    masks = share_ref[members:, :].astype(jnp.bfloat16)
    chosen = chosen_ref[...].astype(jnp.bfloat16)
    across = (((0,), (0,)), ((), ()))
    links = geo_ref[...] * lax.dot_general(masks, chosen, across, preferred_element_type=jnp.float32)
    lam_cols = geo_cols_ref[...] * lax.dot_general(chosen, masks, across, preferred_element_type=jnp.float32)
    mine = near_ref[...] * lax.dot_general(
        masks, mine_ref[...].astype(jnp.bfloat16), across, preferred_element_type=jnp.float32
    )
    left = lax.broadcasted_iota(jnp.int32, (count, LANES), 1) < count
    swapped = pltpu.roll(links, count, 1)
    eye = (
        lax.broadcasted_iota(jnp.int32, (members, members), 0)
        == lax.broadcasted_iota(jnp.int32, (members, members), 1)
    ).astype(jnp.float32)
    zeros = jnp.zeros((members, members), jnp.float32)

    spin = 1.0 / math.sqrt(members - 1.0)

    def begin(block):
        mean = jnp.sum(block, axis=0, keepdims=True) * (1.0 / members)
        return mean, (block - mean) * spin

    mean, apart = begin(picked)
    first, second = apart[:, :count], apart[:, count:]
    own = dot_rows(first, jnp.concatenate([first, eye], axis=1))
    other = dot_rows(first, jnp.concatenate([second * math.sqrt(members - 1.0), eye], axis=1))
    mean = jnp.broadcast_to(jnp.concatenate([mean[:, :count], mean[:, :count]], axis=1), (SUB, LANES))
    for copy in copies:
        copy.wait()
    batch_steps(
        values, variances, 0, count, own, other,
        jnp.where(left, links[:count], 0.0), jnp.where(left, swapped[:count], mine[:count]),
        lam_cols[:count], 0, mean, spin, hist_other, hist_rows, lam_rows, spare,
    )
    moved = dot_rows(hist_rows[:, LANES - members:], hist_other[...])
    after = picked[:, count:] + moved[:, :count]
    change_one = moved[:, count:]

    mean, apart = begin(after)
    own = dot_rows(apart, jnp.concatenate([apart, eye], axis=1))
    other = jnp.concatenate([zeros, own[:, count:]], axis=1)
    mean = jnp.broadcast_to(jnp.concatenate([mean, mean], axis=1), (SUB, LANES))
    batch_steps(
        values, variances, 1, count, own, other,
        jnp.where(left, swapped[count:], 0.0), jnp.where(left, 0.0, mine[count:]),
        lam_cols[count:], count, mean, spin, hist_other, hist_rows, lam_rows, spare,
    )
    change_two = dot_rows(hist_rows[:, LANES - members:], hist_other[:, LANES - members:])
    change_ref[...] = change_one + change_two + dot(change_two, change_one)


def apply_kernel(members, change_ref, mid_ref, core_ref, cross_ref, even_ref, odd_ref, out_hbm, out_ref, sems):
    change = change_ref[...]
    high = change.astype(jnp.bfloat16)
    low = (change - high.astype(jnp.float32)).astype(jnp.bfloat16)
    left = jnp.concatenate([high, high, low], axis=1)
    lane = lax.broadcasted_iota(jnp.int32, (SUB, LANES), 1)
    zone = ((lane + STRIP) & (LANES - 1)) // (2 * STRIP)
    even = (lane % (2 * STRIP) >= STRIP) == (lax.rem(lax.axis_index("lon"), 2) == 0)

    def whole(field, row):
        main = mid_ref[field, row] + core_ref[field, row] + cross_ref[field, row]
        strip = jnp.where(even, even_ref[field, row], odd_ref[field, row])
        parts = []
        for group in range(members // SUB):
            part = main[SUB * group:SUB * (group + 1)] + jnp.where(zone == group, strip, 0.0)
            parts.append(pltpu.roll(part, LANES - 2 * STRIP * group, 1) if group else part)
        return jnp.concatenate(parts, axis=0)

    copies = [pltpu.make_async_copy(out_ref.at[field], out_hbm.at[field], sems.at[field]) for field in range(3)]
    for field in range(3):
        for row in range(0, SUB, 2):
            block = jnp.concatenate([whole(field, row), whole(field, row + 1)], axis=1)
            top = block.astype(jnp.bfloat16)
            rest = (block - top.astype(jnp.float32)).astype(jnp.bfloat16)
            right = jnp.concatenate([top, rest, top], axis=0)
            fresh = block + jnp.dot(left, right, preferred_element_type=jnp.float32)
            for extra in range(2):
                out_ref[field, pl.ds(row + extra, members, stride=SUB), :] = fresh[
                    :, extra * LANES:(extra + 1) * LANES
                ]
        copies[field].start()
    for copy in copies:
        copy.wait()


def closeness(lat_gap, lon_gap, total_cols):
    lon_gap = jnp.abs(lon_gap)
    lon_gap = jnp.minimum(lon_gap, total_cols - lon_gap)
    distance = (lat_gap * lat_gap + lon_gap * lon_gap).astype(jnp.float32)
    return 1.0 / (1.0 + distance / (LOC_RADIUS * LOC_RADIUS))


def body(model_variables, obs_cell, obs_value, obs_variance, tile_mask):
    members = model_variables.shape[1]
    rows_dev = model_variables.shape[2]
    cols_dev = model_variables.shape[3]
    count = obs_cell.shape[1]
    n_lat = lax.axis_size("lat")
    n_lon = lax.axis_size("lon")
    n_tiles = n_lat * n_lon
    lat = lax.axis_index("lat")
    lon = lax.axis_index("lon")
    total_cols = cols_dev * n_lon
    groups = members // SUB
    both = NBATCH * count
    vmem = pl.BlockSpec(memory_space=pltpu.VMEM)
    params = pltpu.CompilerParams(vmem_limit_bytes=VMEM_LIMIT)

    def array(*shape):
        return jax.ShapeDtypeStruct(shape, jnp.float32)

    wide = array(3, rows_dev, members, cols_dev)
    narrow = array(3, rows_dev, SUB, cols_dev)
    base = n_tiles // 4
    core_part, mid_part, cross_part, core_strip, mid_strip, cross_strip, share, seen_cell = pl.pallas_call(
        functools.partial(forecast_kernel, groups, members, n_lat, n_lon),
        out_shape=(wide,) * 3
        + (narrow,) * 3
        + (array(members + base, both), jax.ShapeDtypeStruct((NBATCH, count), jnp.int32)),
        in_specs=[pl.BlockSpec(memory_space=pl.ANY)] * 3,
        out_specs=(pl.BlockSpec(memory_space=pl.ANY),) * 3 + (vmem,) * 5,
        scratch_shapes=[
            pltpu.SMEM((both + PICKS,), jnp.int32),
            pltpu.VMEM((3, 3 * SUB, members + SUB, LANES), jnp.float32),
            pltpu.SMEM((NBATCH, count), jnp.int32),
            pltpu.VMEM((NBATCH, 1, count), jnp.int32),
            pltpu.VMEM((3, members * rows_dev, cols_dev), jnp.float32),
            pltpu.SemaphoreType.DMA((3,)),
            pltpu.SemaphoreType.DMA((3,)),
            pltpu.SemaphoreType.DMA((3, 2)),
        ],
        compiler_params=pltpu.CompilerParams(vmem_limit_bytes=FORECAST_LIMIT),
        name="forecast",
    )(
        obs_cell,
        jnp.swapaxes(tile_mask, 1, 2),
        model_variables.reshape(3, members * rows_dev, cols_dev),
    )

    def swap(x, axis, size, bit):
        return lax.ppermute(x, axis, [(i, i ^ (1 << bit)) for i in range(size)])

    def after(share, *others):
        return lax.optimization_barrier((share,) + others)

    core_pairs = [(i, i ^ 1) for i in range(n_lat)]
    cross_pairs = [p for i in range(1, n_lat - 1, 2) for p in ((i, i + 1), (i + 1, i))]
    even_pairs = [(i, i ^ 1) for i in range(n_lon)]
    odd_pairs = [p for i in range(1, n_lon, 2) for p in ((i, (i + 1) % n_lon), ((i + 1) % n_lon, i))]

    def exchange(x):
        return lax.all_to_all(x, ("lon", "lat"), split_axis=0, concat_axis=0, tiled=True)

    mask_row = jnp.sum(share[members:], axis=0).reshape(1, both)
    pieces = exchange(share[:members].reshape(n_tiles, 1, members * both // n_tiles))
    pieces, cross_strip, core_strip = after(pieces, cross_strip, core_strip)
    cross_corner = lax.ppermute(cross_strip, "lat", cross_pairs)
    core_corner = lax.ppermute(core_strip, "lat", core_pairs)
    piece = jnp.concatenate([jnp.sum(pieces, axis=0), mask_row], axis=1)
    piece, obs_value, obs_variance = after(piece, obs_value, obs_variance)
    seen = jnp.stack([obs_value, obs_variance])
    all_pieces = exchange(jnp.broadcast_to(piece[None], (n_tiles,) + piece.shape))
    strips = mid_strip + core_corner + cross_corner
    all_pieces, strips, cross_part, core_part = after(all_pieces, strips, cross_part, core_part)
    from_cross = lax.ppermute(cross_part, "lat", cross_pairs)
    from_core = lax.ppermute(core_part, "lat", core_pairs)
    from_even = lax.ppermute(strips, "lon", even_pairs)
    from_odd = lax.ppermute(strips, "lon", odd_pairs)
    picked = all_pieces[:, 0, :members * both // n_tiles].reshape(members, both)
    share = jnp.concatenate([picked, all_pieces[:, 0, members * both // n_tiles:]])

    cells = seen_cell.reshape(both)
    obs_row = cells // total_cols
    obs_col = cells % total_cols
    home_lat = obs_row // rows_dev
    home_lon = obs_col // cols_dev
    centre_row = home_lat * rows_dev + rows_dev // 2
    centre_col = home_lon * cols_dev + cols_dev // 2
    geo = closeness(obs_row[:, None] - centre_row, obs_col[:, None] - centre_col, total_cols)
    geo_cols = closeness(obs_row - centre_row[:, None], obs_col - centre_col[:, None], total_cols)
    tiles = jnp.arange(n_tiles, dtype=jnp.int32)
    chosen = (tiles[:, None] == home_lon * n_lat + home_lat).astype(jnp.float32)
    near = closeness(
        obs_row - (lat * rows_dev + rows_dev // 2), obs_col - (lon * cols_dev + cols_dev // 2), total_cols
    )
    near = jnp.broadcast_to(near[:, None], (both, LANES))
    mine = jnp.broadcast_to((tiles == lon * n_lat + lat).astype(jnp.float32)[:, None], (n_tiles, LANES))

    change = pl.pallas_call(
        functools.partial(filter_kernel, count, members),
        out_shape=array(members, members),
        in_specs=[vmem] * 7,
        out_specs=vmem,
        scratch_shapes=[pltpu.VMEM((count, LANES), jnp.float32)] * 2
        + [
            pltpu.VMEM((NBATCH, 2, count, LANES), jnp.float32),
            pltpu.VMEM((NBATCH * count // SUB, 2 * PANEL + 2, SUB, LANES), jnp.float32),
        ]
        + [pltpu.SMEM((NBATCH, count), jnp.float32)] * 2
        + [pltpu.SemaphoreType.DMA((2,))],
        compiler_params=params,
        name="filter",
    )(seen, share, geo, geo_cols, near, chosen, mine)

    out = pl.pallas_call(
        functools.partial(apply_kernel, members),
        out_shape=array(3, members * rows_dev, cols_dev),
        in_specs=[vmem] * 6,
        out_specs=pl.BlockSpec(memory_space=pl.ANY),
        scratch_shapes=[
            pltpu.VMEM((3, members * rows_dev, cols_dev), jnp.float32),
            pltpu.SemaphoreType.DMA((3,)),
        ],
        compiler_params=params,
        name="apply",
    )(change, mid_part, from_core, from_cross, from_even, from_odd)
    return out.reshape(3, members, rows_dev, cols_dev)


def solution(mesh):
    in_specs = (P(None, None, "lat", "lon"), P(), P(), P(), P(None, None, ("lon", "lat")))
    out_specs = P(None, None, "lat", "lon")
    return jax.shard_map(body, mesh=mesh, in_specs=in_specs, out_specs=out_specs, check_vma=False)
```

```python
import functools
import math

import jax
import jax.numpy as jnp
from jax import lax
from jax.experimental import pallas as pl
from jax.experimental.pallas import tpu as pltpu
from jax.sharding import PartitionSpec as P

STEPS = 4
NBATCH = 2
LOC_RADIUS = 256

CORIOLIS = 0.1
COURANT = 0.5
SMALL_EPSILON = 1e-06

SUB = 8
LANES = 128
STRIP = 8
PANEL = 8
PICKS = 4
HIGHEST = lax.Precision.HIGHEST
VMEM_LIMIT = 48 * 1024 * 1024
FORECAST_LIMIT = 53 * 1024 * 1024 + 320 * 1024


def dot_rows(a, b):
    return lax.dot_general(
        a, b, (((0,), (0,)), ((), ())), precision=HIGHEST, preferred_element_type=jnp.float32
    )


def forecast_kernel(
    groups, members, n_lat, n_lon, cell_hbm, mask_hbm, own_hbm,
    core_out, mid_out, cross_out, core_strip, mid_strip, cross_strip, share_ref, cell_out,
    slots, state, cell_ref, mask_ref, own_ref, small_sems, own_sems, out_sems,
):
    lat = lax.axis_index("lat")
    lon = lax.axis_index("lon")
    odd = lax.rem(lat, 2)
    total_rows = n_lat * SUB
    total_cols = n_lon * LANES
    lane = lax.broadcasted_iota(jnp.int32, (SUB, LANES), 1)
    zone = ((lane + STRIP) & (LANES - 1)) // (2 * STRIP)
    at_last = lane % (2 * STRIP) == 2 * STRIP - 1
    at_first = lane % (2 * STRIP) == 0
    scales, turns = [], []
    for row in range(-SUB, 2 * SUB):
        place = lat * SUB + row
        inside = jnp.logical_and(place >= 0, place < total_rows)
        spin = CORIOLIS * ((2.0 * place.astype(jnp.float32) + 1.0) / total_rows - 1.0)
        scales.append(jnp.where(inside, 0.5 * COURANT, 0.0))
        turns.append(jnp.where(inside, spin, 0.0))
    batches, count = cell_ref.shape
    own_copies = [
        pltpu.make_async_copy(own_hbm.at[field], own_ref.at[field], own_sems.at[field]) for field in (1, 2, 0)
    ]
    small = [
        pltpu.make_async_copy(source, target, small_sems.at[place])
        for place, (source, target) in enumerate((
            (cell_hbm, cell_ref), (cell_hbm, cell_out), (mask_hbm, mask_ref)
        ))
    ]
    for copy in own_copies + small:
        copy.start()

    def minus(a, b):
        if b is None:
            return a
        return -b if a is None else a - b

    def plus(a, b):
        if a is None or b is None:
            return b if a is None else a
        return a + b

    def times(scale, a):
        return None if a is None else scale * a

    def along(x):
        if x is None:
            return None
        right, left = pltpu.roll(x, LANES - 1, 1), pltpu.roll(x, 1, 1)
        rights = [right[SUB * g:SUB * (g + 1)] for g in range(groups + 1)]
        lefts = [left[SUB * g:SUB * (g + 1)] for g in range(groups + 1)]
        first, last = rights[0], lefts[0]
        for g in range(1, groups):
            first = jnp.where(zone == g, rights[g], first)
            last = jnp.where(zone == g, lefts[g], last)
        mend = jnp.where(at_last, rights[groups] - first, jnp.where(at_first, last - lefts[groups], 0.0))
        parts = [rights[g] - lefts[g] + jnp.where(zone == g, mend, 0.0) for g in range(groups)]
        parts.append(
            jnp.where(at_last, first, rights[groups]) - jnp.where(at_first, last, lefts[groups])
        )
        return jnp.concatenate(parts, axis=0)

    live = [dict() for _ in range(3)]

    def get(field, row):
        return state[field, row + SUB] if row in live[field] else None

    def put(field, row, value):
        if value is not None:
            live[field][row] = True
            state[field, row + SUB] = value

    def list_cells(start, stop, found):
        for index in range(start, stop):
            cell = cell_ref[index // count, index % count]
            row = lax.div(cell, total_cols)
            col = cell - row * total_cols - lon * LANES
            row = row - lat * SUB + SUB
            col = jnp.where(col < 0, col + total_cols, col)
            west = col >= total_cols - STRIP
            near = jnp.logical_and(row > 0, row < 3 * SUB - 1)
            near = jnp.logical_and(near, jnp.logical_or(col < LANES + STRIP, west))
            ring = jnp.where(west, col + (2 * LANES - total_cols), col)
            slots[found] = (row * (2 * LANES) + ring) * LANES + index
            found = found + near.astype(jnp.int32)
        return found

    for copy in small:
        copy.wait()
    for field, copy in zip((1, 2, 0), own_copies):
        copy.wait()
        for row in range(SUB):
            pieces = [
                own_ref[field, pl.ds(group * SUB * SUB + row, SUB, stride=SUB), :] for group in range(groups)
            ]
            pieces = [pieces[0]] + [pltpu.roll(pieces[g], 2 * STRIP * g, 1) for g in range(1, groups)]
            put(field, row, jnp.concatenate(pieces + [jnp.zeros((SUB, LANES), jnp.float32)], axis=0))

    cells = batches * count
    part_rows = [2 * SUB - 2 * SUB * odd, SUB, 2 * SUB * odd]
    outs = [core_out, mid_out, cross_out]

    def out_copy(part, fields):
        rows = pl.ds(part_rows[part], SUB)
        return pltpu.make_async_copy(
            state.at[fields, rows, pl.ds(0, members)], outs[part].at[fields],
            out_sems.at[part, 0 if fields.size == 1 else 1],
        )

    for row in (-SUB, 2 * SUB - 1):
        for field in range(2):
            state[field, row + SUB] = jnp.zeros((members + SUB, LANES), jnp.float32)
    found = jnp.int32(0)
    for step in range(STEPS):
        for row in range(-SUB, 2 * SUB):
            slope = plus(along(get(1, row)), minus(get(2, row + 1), get(2, row - 1)))
            put(0, row, minus(get(0, row), times(scales[row + SUB], slope)))
        found = list_cells(cells * step // STEPS, cells * (step + 1) // STEPS, found)
        if step == STEPS - 1:
            for part in range(3):
                out_copy(part, pl.ds(0, 1)).start()
        for row in range(-SUB, 2 * SUB):
            east, north = get(1, row), get(2, row)
            slope = minus(get(0, row + 1), get(0, row - 1))
            put(1, row, minus(plus(east, times(turns[row + SUB], north)), times(scales[row + SUB], along(get(0, row)))))
            put(2, row, minus(minus(north, times(turns[row + SUB], east)), times(scales[row + SUB], slope)))
    for part in range(3):
        out_copy(part, pl.ds(1, 2)).start()

    halo = pl.ds(members, SUB)
    for field in range(3):
        up, down = state[field, pl.ds(0, SUB), halo, :], state[field, pl.ds(2 * SUB, SUB), halo, :]
        mid_strip[field] = state[field, pl.ds(SUB, SUB), halo, :]
        core_strip[field] = jnp.where(odd == 1, up, down)
        cross_strip[field] = jnp.where(odd == 1, down, up)
    tiles = share_ref.shape[0] - members
    mine = lax.broadcasted_iota(jnp.int32, (tiles, LANES), 0) == lax.rem(lon * n_lat + lat, tiles)
    mask = jnp.concatenate([mask_ref[batch] for batch in range(batches)], axis=1).astype(jnp.float32)
    share_ref[members:, :] = jnp.where(mine, mask, 0.0)
    wide = lax.broadcasted_iota(jnp.int32, (members, LANES), 1)

    def pick(turn, share):
        for extra in range(PICKS):
            item = turn * PICKS + extra
            packed = jnp.where(item < found, slots[item], 0)
            index = packed & (LANES - 1)
            ring = (packed >> 7) & (2 * LANES - 1)
            row = packed >> 15
            pieces = []
            for group in range(groups):
                place = pl.multiple_of(jnp.where(ring < LANES, group * SUB, members), SUB)
                piece = state[0, row, pl.ds(place, SUB), :]
                pieces.append(pltpu.roll(piece, (index - ring - 2 * STRIP * group) & (LANES - 1), 1))
            turned = jnp.concatenate(pieces, axis=0)
            share = jnp.where(wide == jnp.where(item < found, index, LANES), turned, share)
        return share

    share_ref[:members, :] = lax.fori_loop(
        0, lax.div(found + PICKS - 1, PICKS), pick, jnp.zeros((members, LANES), jnp.float32)
    )
    for part in range(3):
        out_copy(part, pl.ds(0, 1)).wait()
        out_copy(part, pl.ds(1, 2)).wait()


def batch_steps(
    values, variances, batch, count, own, other, lam_own, lam_other, lam_cols, offset, mean, spin,
    hist_other, hist_rows, lam_rows, spare,
):
    groups = count // SUB
    own = [own[SUB * i:SUB * (i + 1)] for i in range(groups)]
    other = [other[SUB * i:SUB * (i + 1)] for i in range(groups)]

    lam_rows[batch, 0] = lam_own
    lam_rows[batch, 1] = lam_other

    def lam_row(side, k):
        return jnp.broadcast_to(lam_rows[batch, side, k:k + 1, :], (SUB, LANES))

    def column(x, lane):
        return jnp.broadcast_to(x[:, lane:lane + 1], (SUB, LANES))

    ready = None
    for first in range(0, count, PANEL):
        home, base = divmod(first, SUB)
        live = range(home, groups)
        inside = range(PANEL)
        close = live[:2]
        cols = [{i: column(own[i], first + q) for i in close} for q in inside]
        if ready is not None:
            for q in inside:
                cols[q][home] = ready[q]
        lams = [
            {i: column(lam_cols[SUB * i:SUB * (i + 1)], offset + first + q) for i in close} for q in inside
        ]
        place = batch * groups + home

        def keep(slot, x):
            spare[place, slot] = x

        def spread(slot, row):
            return jnp.broadcast_to(spare[place, slot, row:row + 1, :], (SUB, LANES))

        for q in inside:
            keep(q, cols[q][home])
        keep(2 * PANEL, own[home])
        keep(2 * PANEL + 1, other[home])
        for q in inside:
            keep(PANEL + q, lams[q][home])
        ahead = home + 1 < groups
        if ahead:
            keep(2 * PANEL + 2, lams[PANEL - 1][home + 1])
        block = {(a, b): spread(b, base + a) for a in inside for b in inside if a <= b}
        rows_own = [spread(2 * PANEL, base + q) for q in inside]
        rows_other = [spread(2 * PANEL + 1, base + q) for q in inside]
        means = [column(mean, first + q) for q in inside]
        noises = [jnp.full((SUB, LANES), variances[batch, first + q], jnp.float32) for q in inside]
        total = block[0, 0] + (noises[0] + SMALL_EPSILON)
        taken = []

        def follow(i, t, now, links, kept):
            shrink, alpha, beta, first_own, second_own, first_other, second_other = taken[t]
            g = now[t]
            u = links[t] * g
            scaled = shrink * u
            for q in range(t + 1, PANEL):
                kept[q][i] = now[q] + (g * alpha[q] + scaled * beta[q])
            own[i] = own[i] + (g * first_own + u * second_own)
            other[i] = other[i] + (g * first_other + u * second_other)

        for t in inside:
            k = first + t
            noise = noises[t] * lax.rsqrt(noises[t])
            square = block[t, t]
            root = lax.rsqrt(total)
            inverse = root * root
            below = 1.0 + noise * root
            guess = pl.reciprocal(below, approx=True)
            shrink = (inverse * guess) * (below * guess - 2.0)
            shift = (values[batch, k] - means[t]) * inverse
            row_own, row_other = rows_own[t], rows_other[t]
            seen_own = lam_row(0, k) * row_own
            seen_other = lam_row(1, k) * row_other
            hist_other[k:k + 1, :] = seen_other[:1]
            hist_rows[k:k + 1, :] = (shift * spin + shrink * row_own)[:1]
            mean = mean + shift * seen_own
            first_own = shrink * seen_own
            second_own = shrink * (row_own + square * first_own)
            first_other = shrink * seen_other
            second_other = shrink * (row_other + square * first_other)
            alpha, beta = {}, {}
            if t + 1 < PANEL:
                linked = spread(PANEL + t, base + t + 1) * block[t, t + 1]
                flat = block[t + 1, t + 1] + (noises[t + 1] + SMALL_EPSILON)
                total = flat + shrink * (2.0 * (linked * block[t, t + 1]) + shrink * (linked * linked * square))
            for q in range(t + 1, PANEL):
                linked = spread(PANEL + t, base + q) * block[t, q]
                alpha[q] = shrink * linked
                beta[q] = block[t, q] + square * alpha[q]
                rows_own[q] = rows_own[q] + (block[t, q] * first_own + linked * second_own)
                rows_other[q] = rows_other[q] + (block[t, q] * first_other + linked * second_other)
                means[q] = means[q] + shift * linked
            for a in range(t + 1, PANEL):
                for b in range(a, PANEL):
                    block[a, b] = (block[a, b] + alpha[b] * block[t, a]) + alpha[a] * beta[b]
            if ahead and t == PANEL - 1:
                g = cols[t][home + 1]
                scaled = shrink * (lams[t][home + 1] * g)
                for q in inside:
                    v = shrink * (spread(2 * PANEL + 2, q) * edge[q])
                    ready[q] = ready[q] + (g * v + scaled * (edge[q] + square * v))
            taken.append((shrink, alpha, beta, first_own, second_own, first_other, second_other))
            for i in close[1:]:
                follow(i, t, [col[i] for col in cols], [lam[i] for lam in lams], cols)
            if ahead and t == PANEL - 2:
                ready = [column(own[home + 1], first + PANEL + q) for q in inside]
                edge = [column(rows_own[t + 1], first + PANEL + q) for q in inside]
        for i in live[2:]:
            far_cols = [{i: column(own[i], first + q)} for q in inside]
            far_lams = [column(lam_cols[SUB * i:SUB * (i + 1)], offset + first + q) for q in inside]
            for t in inside:
                follow(i, t, [col[i] for col in far_cols], far_lams, far_cols)


def filter_kernel(
    count, members, seen_ref, share_ref, geo_ref, geo_cols_ref, near_ref, chosen_ref, mine_ref,
    change_ref, hist_other, hist_rows, lam_rows, spare, values, variances, sems,
):
    copies = [
        pltpu.make_async_copy(seen_ref.at[0], values, sems.at[0]),
        pltpu.make_async_copy(seen_ref.at[1], variances, sems.at[1]),
    ]
    for copy in copies:
        copy.start()
    picked = share_ref[:members, :]
    masks = share_ref[members:, :].astype(jnp.bfloat16)
    chosen = chosen_ref[...].astype(jnp.bfloat16)
    across = (((0,), (0,)), ((), ()))
    links = geo_ref[...] * lax.dot_general(masks, chosen, across, preferred_element_type=jnp.float32)
    lam_cols = geo_cols_ref[...] * lax.dot_general(chosen, masks, across, preferred_element_type=jnp.float32)
    mine = near_ref[...] * lax.dot_general(
        masks, mine_ref[...].astype(jnp.bfloat16), across, preferred_element_type=jnp.float32
    )
    left = lax.broadcasted_iota(jnp.int32, (count, LANES), 1) < count
    swapped = pltpu.roll(links, count, 1)
    eye = (
        lax.broadcasted_iota(jnp.int32, (members, members), 0)
        == lax.broadcasted_iota(jnp.int32, (members, members), 1)
    ).astype(jnp.float32)
    zeros = jnp.zeros((members, members), jnp.float32)

    spin = 1.0 / math.sqrt(members - 1.0)

    def begin(block):
        mean = jnp.sum(block, axis=0, keepdims=True) * (1.0 / members)
        return mean, (block - mean) * spin

    mean, apart = begin(picked)
    first, second = apart[:, :count], apart[:, count:]
    rows = dot_rows(first, jnp.concatenate([first, eye, second * math.sqrt(members - 1.0), eye], axis=1))
    own, other = rows[:, :LANES], rows[:, LANES:]
    mean = jnp.broadcast_to(jnp.concatenate([mean[:, :count], mean[:, :count]], axis=1), (SUB, LANES))
    for copy in copies:
        copy.wait()
    batch_steps(
        values, variances, 0, count, own, other,
        jnp.where(left, links[:count], 0.0), jnp.where(left, swapped[:count], mine[:count]),
        lam_cols[:count], 0, mean, spin, hist_other, hist_rows, lam_rows, spare,
    )
    moved = dot_rows(hist_rows[:, LANES - members:], hist_other[...])
    after = picked[:, count:] + moved[:, :count]
    change_one = moved[:, count:]

    mean, apart = begin(after)
    rows = dot_rows(apart, jnp.concatenate([apart, eye, zeros, eye + change_one], axis=1))
    own, other = rows[:, :LANES], rows[:, LANES:]
    mean = jnp.broadcast_to(jnp.concatenate([mean, mean], axis=1), (SUB, LANES))
    batch_steps(
        values, variances, 1, count, own, other,
        jnp.where(left, swapped[count:], 0.0), jnp.where(left, 0.0, mine[count:]),
        lam_cols[count:], count, mean, spin, hist_other, hist_rows, lam_rows, spare,
    )
    change_ref[...] = change_one + dot_rows(hist_rows[:, LANES - members:], hist_other[:, LANES - members:])


def apply_kernel(members, change_ref, mid_ref, core_ref, cross_ref, even_ref, odd_ref, out_hbm, out_ref, sems):
    change = change_ref[...]
    high = change.astype(jnp.bfloat16)
    low = (change - high.astype(jnp.float32)).astype(jnp.bfloat16)
    left = jnp.concatenate([high, high, low], axis=1)
    lane = lax.broadcasted_iota(jnp.int32, (SUB, LANES), 1)
    zone = ((lane + STRIP) & (LANES - 1)) // (2 * STRIP)
    even = (lane % (2 * STRIP) >= STRIP) == (lax.rem(lax.axis_index("lon"), 2) == 0)

    def whole(field, row):
        main = mid_ref[field, row] + core_ref[field, row] + cross_ref[field, row]
        strip = jnp.where(even, even_ref[field, row], odd_ref[field, row])
        parts = []
        for group in range(members // SUB):
            part = main[SUB * group:SUB * (group + 1)] + jnp.where(zone == group, strip, 0.0)
            parts.append(pltpu.roll(part, LANES - 2 * STRIP * group, 1) if group else part)
        return jnp.concatenate(parts, axis=0)

    copies = [pltpu.make_async_copy(out_ref.at[field], out_hbm.at[field], sems.at[field]) for field in range(3)]
    for field in range(3):
        for row in range(0, SUB, 2):
            block = jnp.concatenate([whole(field, row), whole(field, row + 1)], axis=1)
            top = block.astype(jnp.bfloat16)
            rest = (block - top.astype(jnp.float32)).astype(jnp.bfloat16)
            right = jnp.concatenate([top, rest, top], axis=0)
            fresh = block + jnp.dot(left, right, preferred_element_type=jnp.float32)
            for extra in range(2):
                out_ref[field, pl.ds(row + extra, members, stride=SUB), :] = fresh[
                    :, extra * LANES:(extra + 1) * LANES
                ]
        copies[field].start()
    for copy in copies:
        copy.wait()


def closeness(lat_gap, lon_gap, total_cols):
    lon_gap = jnp.abs(lon_gap)
    lon_gap = jnp.minimum(lon_gap, total_cols - lon_gap)
    distance = (lat_gap * lat_gap + lon_gap * lon_gap).astype(jnp.float32)
    return 1.0 / (1.0 + distance / (LOC_RADIUS * LOC_RADIUS))


def body(model_variables, obs_cell, obs_value, obs_variance, tile_mask):
    members = model_variables.shape[1]
    rows_dev = model_variables.shape[2]
    cols_dev = model_variables.shape[3]
    count = obs_cell.shape[1]
    n_lat = lax.axis_size("lat")
    n_lon = lax.axis_size("lon")
    n_tiles = n_lat * n_lon
    lat = lax.axis_index("lat")
    lon = lax.axis_index("lon")
    total_cols = cols_dev * n_lon
    groups = members // SUB
    both = NBATCH * count
    vmem = pl.BlockSpec(memory_space=pltpu.VMEM)
    params = pltpu.CompilerParams(vmem_limit_bytes=VMEM_LIMIT)

    def array(*shape):
        return jax.ShapeDtypeStruct(shape, jnp.float32)

    wide = array(3, rows_dev, members, cols_dev)
    narrow = array(3, rows_dev, SUB, cols_dev)
    base = n_tiles // 4
    core_part, mid_part, cross_part, core_strip, mid_strip, cross_strip, share, seen_cell = pl.pallas_call(
        functools.partial(forecast_kernel, groups, members, n_lat, n_lon),
        out_shape=(wide,) * 3
        + (narrow,) * 3
        + (array(members + base, both), jax.ShapeDtypeStruct((NBATCH, count), jnp.int32)),
        in_specs=[pl.BlockSpec(memory_space=pl.ANY)] * 3,
        out_specs=(pl.BlockSpec(memory_space=pl.ANY),) * 3 + (vmem,) * 5,
        scratch_shapes=[
            pltpu.SMEM((both + PICKS,), jnp.int32),
            pltpu.VMEM((3, 3 * SUB, members + SUB, LANES), jnp.float32),
            pltpu.SMEM((NBATCH, count), jnp.int32),
            pltpu.VMEM((NBATCH, 1, count), jnp.int32),
            pltpu.VMEM((3, members * rows_dev, cols_dev), jnp.float32),
            pltpu.SemaphoreType.DMA((3,)),
            pltpu.SemaphoreType.DMA((3,)),
            pltpu.SemaphoreType.DMA((3, 2)),
        ],
        compiler_params=pltpu.CompilerParams(vmem_limit_bytes=FORECAST_LIMIT),
        name="forecast",
    )(
        obs_cell,
        jnp.swapaxes(tile_mask, 1, 2),
        model_variables.reshape(3, members * rows_dev, cols_dev),
    )

    def swap(x, axis, size, bit):
        return lax.ppermute(x, axis, [(i, i ^ (1 << bit)) for i in range(size)])

    def after(share, *others):
        return lax.optimization_barrier((share,) + others)

    core_pairs = [(i, i ^ 1) for i in range(n_lat)]
    cross_pairs = [p for i in range(1, n_lat - 1, 2) for p in ((i, i + 1), (i + 1, i))]
    even_pairs = [(i, i ^ 1) for i in range(n_lon)]
    odd_pairs = [p for i in range(1, n_lon, 2) for p in ((i, (i + 1) % n_lon), ((i + 1) % n_lon, i))]

    cross_corner = lax.ppermute(cross_strip, "lat", cross_pairs)
    lat_bits = n_lat.bit_length() - 1
    lon_bits = n_lon.bit_length() - 1
    for bit in reversed(range(1, lat_bits)):
        share = share + swap(share, "lat", n_lat, bit)
    corner_rows = core_strip.size // both
    message = jnp.concatenate([share, core_strip.reshape(corner_rows, both)])
    message = lax.ppermute(message, "lat", core_pairs)
    share = share + message[:share.shape[0]]
    core_corner = message[share.shape[0]:].reshape(core_strip.shape)
    share, cross_part, obs_value, obs_variance = after(share, cross_part, obs_value, obs_variance)
    from_cross = lax.ppermute(cross_part, "lat", cross_pairs)
    seen = jnp.stack([obs_value, obs_variance])
    strips = mid_strip + core_corner + cross_corner
    for bit in range(lon_bits):
        if bit == lon_bits - 2:
            share, core_part, seen = after(share, core_part, seen)
            from_core = lax.ppermute(core_part, "lat", core_pairs)
        if bit == lon_bits - 1:
            share, strips = after(share, strips)
            from_even = lax.ppermute(strips, "lon", even_pairs)
            from_odd = lax.ppermute(strips, "lon", odd_pairs)
        other = swap(share, "lon", n_lon, bit)
        if bit < lon_bits - 2:
            share = share + other
        else:
            high = (lon >> bit) & 1
            mine, theirs = share[members:], other[members:]
            share = jnp.concatenate([
                share[:members] + other[:members],
                jnp.where(high == 1, theirs, mine),
                jnp.where(high == 1, mine, theirs),
            ])

    cells = seen_cell.reshape(both)
    obs_row = cells // total_cols
    obs_col = cells % total_cols
    home_lat = obs_row // rows_dev
    home_lon = obs_col // cols_dev
    centre_row = home_lat * rows_dev + rows_dev // 2
    centre_col = home_lon * cols_dev + cols_dev // 2
    geo = closeness(obs_row[:, None] - centre_row, obs_col[:, None] - centre_col, total_cols)
    geo_cols = closeness(obs_row - centre_row[:, None], obs_col - centre_col[:, None], total_cols)
    tiles = jnp.arange(n_tiles, dtype=jnp.int32)
    chosen = (tiles[:, None] == home_lon * n_lat + home_lat).astype(jnp.float32)
    near = closeness(
        obs_row - (lat * rows_dev + rows_dev // 2), obs_col - (lon * cols_dev + cols_dev // 2), total_cols
    )
    near = jnp.broadcast_to(near[:, None], (both, LANES))
    mine = jnp.broadcast_to((tiles == lon * n_lat + lat).astype(jnp.float32)[:, None], (n_tiles, LANES))

    change = pl.pallas_call(
        functools.partial(filter_kernel, count, members),
        out_shape=array(members, members),
        in_specs=[vmem] * 7,
        out_specs=vmem,
        scratch_shapes=[pltpu.VMEM((count, LANES), jnp.float32)] * 2
        + [
            pltpu.VMEM((NBATCH, 2, count, LANES), jnp.float32),
            pltpu.VMEM((NBATCH * count // SUB, 2 * PANEL + 3, SUB, LANES), jnp.float32),
        ]
        + [pltpu.SMEM((NBATCH, count), jnp.float32)] * 2
        + [pltpu.SemaphoreType.DMA((2,))],
        compiler_params=params,
        name="filter",
    )(seen, share, geo, geo_cols, near, chosen, mine)

    out = pl.pallas_call(
        functools.partial(apply_kernel, members),
        out_shape=array(3, members * rows_dev, cols_dev),
        in_specs=[vmem] * 6,
        out_specs=pl.BlockSpec(memory_space=pl.ANY),
        scratch_shapes=[
            pltpu.VMEM((3, members * rows_dev, cols_dev), jnp.float32),
            pltpu.SemaphoreType.DMA((3,)),
        ],
        compiler_params=params,
        name="apply",
    )(change, mid_part, from_core, from_cross, from_even, from_odd)
    return out.reshape(3, members, rows_dev, cols_dev)


def solution(mesh):
    in_specs = (P(None, None, "lat", "lon"), P(), P(), P(), P(None, None, ("lon", "lat")))
    out_specs = P(None, None, "lat", "lon")
    return jax.shard_map(body, mesh=mesh, in_specs=in_specs, out_specs=out_specs, check_vma=False)
```
